32 devices in a mesh: dp: 4 (over z), slab: 4 (over x, core), chan: 2 (over y).
Axes of the slice: x: 2, y: 2, z: 4, core: 2. Of those that a mesh axis runs over, the one named last changes fastest.
Arguments:
- volumes: bfloat16 [4, 8, 32, 16, 256], P('dp', 'slab', None, None, 'chan'), may hold values from -6 to 6
- weight: bfloat16 [3, 3, 3, 256, 256], P(None, None, None, 'chan'), may hold values from -0.078125 to 0.078125
- bias: bfloat16 [256], P('chan'), may hold values from -3 to 3
- cotangent: bfloat16 [4, 8, 32, 16, 256], P('dp', 'slab', None, None, 'chan'), may hold values from -6 to 6
Outputs:
- activations: bfloat16 [4, 8, 32, 16, 256], P('dp', 'slab', None, None, 'chan')
- input_grad: bfloat16 [4, 8, 32, 16, 256], P('dp', 'slab', None, None, 'chan')
- weight_grad: float32 [3, 3, 3, 256, 256], P(None, None, None, 'chan')
- bias_grad: float32 [256], P('chan')
The draws below stay inside these ranges and needn't reach their ends.
All inputs are finite; a program needn't handle non-finite values.
Results may differ from the reference program's by a relative error of at most 0.0049.
Values may be sent and summed in bfloat16 or wider, within the bound.
No kernel may reach another device: no remote copies, remote signals or barrier semaphores. Data moves between devices by JAX's collectives and lax.ppermute only.
A program may use at most 64 MiB of HBM per device.

```python
import jax
import jax.numpy as jnp
from jax import lax

CIN = 256
COUT = 256
PX = 32
PY = 16
BATCH = 4
NZ = 8


def block_levels(stream_key, dims, cuts, smallest, largest):
    level, own = 1.0, jax.random.fold_in(stream_key, 6)
    for axis_at, blocks in cuts:
        heights = jnp.exp(jax.random.uniform(jax.random.fold_in(own, axis_at), (blocks,), jnp.float32, smallest / len(cuts), largest / len(cuts)))
        level = level * jnp.repeat(heights, dims[axis_at] // blocks).reshape([-1 if axis == axis_at else 1 for axis in range(len(dims))])
    return level


def gaussian(own_key, shape, scale, reach, split=(), held_as=jnp.bfloat16):
    drawn = scale * jax.random.normal(own_key, shape, jnp.float32)
    if split:
        drawn = drawn * block_levels(own_key, shape, split, -0.22, 0.18)
    return jnp.clip(drawn, -reach, reach).astype(held_as)


def setup_inputs(seed: int = 0) -> dict:
    splits = jax.random.split(jax.random.key(seed), 5)
    volumes = gaussian(splits[0], (BATCH, NZ, PX, PY, CIN), 1.0, 6.0, ((0, 4), (1, 4), (4, 2)))
    weight = gaussian(splits[1], (3, 3, 3, CIN, COUT), (27 * CIN) ** -0.5, 0.078125, ((3, 2),))
    bias = gaussian(splits[2], (COUT,), 0.5, 3.0, ((0, 2),))
    cotangent = gaussian(splits[3], (BATCH, NZ, PX, PY, COUT), 1.0, 6.0, ((0, 4), (1, 4), (4, 2)))
    return dict(volumes=volumes, weight=weight, bias=bias, cotangent=cotangent)


def convolve(field, kernel):
    return lax.conv_general_dilated(field, kernel, (1, 1, 1), 'SAME', dimension_numbers=('NDHWC', 'DHWIO', 'NDHWC'), precision=lax.Precision.HIGHEST)

def reference(volumes, weight, bias, cotangent):
    field = volumes.astype(jnp.float32)
    kernel = weight.astype(jnp.float32)
    summed, backward = jax.vjp(convolve, field, kernel)
    pre = summed + bias.astype(jnp.float32)
    logistic = jax.nn.sigmoid(pre)
    activations = (pre * logistic).astype(jnp.bfloat16)
    grad_pre = (cotangent.astype(jnp.float32) * logistic * (1.0 + pre * (1.0 - logistic))).astype(jnp.bfloat16)
    field_grad, kernel_grad = backward(grad_pre.astype(jnp.float32))
    factor = (BATCH * NZ * PX * PY) ** (-0.5)
    weight_grad = kernel_grad * factor
    bias_grad = lax.optimization_barrier(jnp.sum(grad_pre.astype(jnp.float32), axis=(0, 1, 2, 3))) * factor
    return (activations, field_grad.astype(jnp.bfloat16), weight_grad, bias_grad)
```

```python
import functools

import jax
import jax.numpy as jnp
from jax import lax
from jax.experimental import pallas as pl
from jax.experimental.pallas import tpu as pltpu
from jax.sharding import PartitionSpec as P

BF = jnp.bfloat16
F32 = jnp.float32
MIB = 1 << 20


def swap(value, axis, bit):
    return lax.ppermute(value, axis, [(i, i ^ bit) for i in range(lax.axis_size(axis))])


def vmem_call(body, outs, scratch, flops, *args, limit=40):
    shapes = [jax.ShapeDtypeStruct(s, d) for s, d in outs]
    moved = sum(a.size * a.dtype.itemsize for a in args)
    return pl.pallas_call(
        body,
        out_shape=shapes,
        in_specs=[pl.BlockSpec(memory_space=pltpu.SMEM)]
        + [pl.BlockSpec(memory_space=pltpu.VMEM)] * (len(args) - 1),
        out_specs=[pl.BlockSpec(memory_space=pltpu.VMEM)] * len(shapes),
        scratch_shapes=scratch,
        compiler_params=pltpu.CompilerParams(vmem_limit_bytes=limit * MIB),
        cost_estimate=pl.CostEstimate(flops=flops, bytes_accessed=moved, transcendentals=0),
    )(*args)


def shift_y(value, step, ny):
    rows = value.shape[0]
    y = lax.broadcasted_iota(jnp.int32, value.shape, 0) % ny
    rolled = pltpu.roll(value, (-step) % rows, 0)
    return jnp.where(y == (0 if step < 0 else ny - 1), 0.0, rolled)


def put_plane(buf, at, value, ny, flip):
    cells, lanes = value.shape
    wide = value.astype(F32)
    edge = jnp.zeros((ny, 3 * lanes), BF)
    buf[at, 0:ny, :] = edge
    buf[at, ny + cells : 2 * ny + cells, :] = edge
    for c in range(3):
        step = (1 - c) if flip else (c - 1)
        moved = value if step == 0 else shift_y(wide, step, ny).astype(BF)
        buf[at, ny : ny + cells, c * lanes : (c + 1) * lanes] = moved


def forward_body(ny, pos, vol, near, far, w, own, send, buf):
    planes, cells, _ = vol.shape
    odd, y = pos[0], pos[1]
    for p in range(planes):
        put_plane(buf, p + 1, vol[p], ny, False)
    put_plane(buf, jnp.where(odd == 0, planes + 1, 0), near[...], ny, False)
    put_plane(buf, jnp.where(odd == 0, 0, planes + 1), far[...], ny, False)
    half = own.shape[1]
    for z in range(planes):
        acc = jnp.zeros((cells, 2 * half), F32)
        for a in range(3):
            lhs = jnp.concatenate([buf[z + a, b * ny : b * ny + cells, :] for b in range(3)], axis=1)
            acc = acc + jnp.dot(lhs, w[a], preferred_element_type=F32)
        own[z * cells : (z + 1) * cells, :] = jnp.where(y == 0, acc[:, :half], acc[:, half:])
        send[z * cells : (z + 1) * cells, :] = jnp.where(y == 0, acc[:, half:], acc[:, :half]).astype(BF)


def gate_body(pos, own, recv, bias, cot, act, grad):
    pre = own[...] + recv[...].astype(F32) + bias[...].astype(F32)
    s = 1.0 / (1.0 + jnp.exp(-pre))
    act[...] = (pre * s).astype(BF)
    grad[...] = (cot[...].astype(F32) * s * (1.0 + pre * (1.0 - s))).astype(BF)


def volume_body(pos, v0, v1, v2, ends, vt):
    planes, cells, lanes = v0.shape
    mine, k = pos[2], pos[3]
    keep = lanes // 2
    total = 4 * planes

    def put(at, value):
        turned = value.astype(F32).T
        turned = jnp.where(k == 0, turned[:keep], turned[keep:]).astype(BF)
        for a in range(3):
            vt[at + 2 - a, a * keep : (a + 1) * keep, :] = turned

    put(-1 + 1, ends[0])
    put(total + 1, ends[1])
    for p in range(planes):
        put(mine * planes + p + 1, v0[p])
        put((mine ^ 2) * planes + p + 1, v1[p])
        put((mine ^ 1) * planes + p + 1, v2[p])
        put((mine ^ 3) * planes + p + 1, v2[planes + p])


def kernel_body(ny, pos, vt, g0, g1, g2, keep1, send1, total, buf, acc):
    planes, cells = g0.shape[0], g0.shape[1]
    mine, bit0 = pos[2], pos[4]
    bsum = jnp.zeros((1, g0.shape[2]), F32)
    for p in range(planes):
        for at, value in (
            (mine * planes + p, g0[p]),
            ((mine ^ 2) * planes + p, g1[p]),
            ((mine ^ 1) * planes + p, g2[p]),
            ((mine ^ 3) * planes + p, g2[planes + p]),
        ):
            put_plane(buf, at, value, ny, True)
            bsum = bsum + jnp.sum(value.astype(F32), axis=0, keepdims=True)
    total[...] = jnp.broadcast_to(bsum, total.shape)
    rows = acc.shape[0]
    for b in range(3):
        summed = jnp.zeros(acc.shape, F32)
        for z in range(4 * planes):
            rhs = buf[z, (2 - b) * ny : (2 - b) * ny + cells, :]
            summed = summed + jnp.dot(vt[z + 2], rhs, preferred_element_type=F32)
        acc[...] = summed
        part = rows // 6
        for a in range(3):
            at = (3 * b + a) * part
            keep1[at : at + part, :] = acc[pl.ds((2 * a + bit0) * part, part), :]
            send1[at : at + part, :] = acc[pl.ds((2 * a + 1 - bit0) * part, part), :].astype(BF)
    send1[9 * part : 9 * part + 16, :] = split_rows(total)


def split_rows(total):
    value = jnp.broadcast_to(total[0:1, :], (16, total.shape[1]))
    high = value.astype(BF)
    rest = value - high.astype(F32)
    mid = rest.astype(BF)
    low = (rest - mid.astype(F32)).astype(BF)
    return jnp.concatenate([high, mid, low], axis=1)


def joined(rows):
    n = rows.shape[1] // 3
    wide = rows[0:8, :].astype(F32)
    return wide[:, :n] + wide[:, n : 2 * n] + wide[:, 2 * n :]


def second_body(pos, keep1, recv1, total1, keep2, send2, total2):
    bit1 = pos[5]
    part = keep2.shape[0] // 9
    total2[...] = total1[...] + joined(recv1[18 * part : 18 * part + 16, :])
    for n in range(9):
        lo = keep1[2 * n * part : (2 * n + 1) * part, :] + recv1[2 * n * part : (2 * n + 1) * part, :].astype(F32)
        hi = keep1[(2 * n + 1) * part : (2 * n + 2) * part, :] + recv1[
            (2 * n + 1) * part : (2 * n + 2) * part, :
        ].astype(F32)
        keep2[n * part : (n + 1) * part, :] = jnp.where(bit1 == 0, lo, hi)
        send2[n * part : (n + 1) * part, :] = jnp.where(bit1 == 0, hi, lo).astype(BF)
    send2[9 * part : 9 * part + 16, :] = split_rows(total2)


def last_body(factor, pos, keep2, recv2, total2, quarter, total3):
    rows = keep2.shape[0]
    total3[...] = (total2[...] + joined(recv2[rows : rows + 16, :])) * factor
    quarter[0:rows, :] = ((keep2[...] + recv2[0:rows, :].astype(F32)) * factor).astype(BF)
    quarter[rows : rows + 16, :] = split_rows(total3)


def spread_body(pos, d, dx, e, total3, out, bias_out):
    x, y, k, bit0, bit1 = pos[6], pos[1], pos[3], pos[4], pos[5]
    half = out.shape[4] // 2
    for piece, kk, xx in ((d, k, x), (dx, k, 1 - x), (e.at[0], 1 - k, x), (e.at[1], 1 - k, 1 - x)):
        for j in range(4):
            q = 2 * (bit0 ^ (j >> 1)) + (bit1 ^ (j & 1))
            row = pl.multiple_of(kk * 64 + q * 16, 16)
            lane = pl.multiple_of(xx * half, half)
            n = 3 * pl.program_id(1) + pl.program_id(0)
            for c in range(3):
                out[0, 0, c, pl.ds(row, 16), pl.ds(lane, half)] = piece[
                    j, pl.ds(pl.multiple_of(n * 16, 16), 16), c * half : (c + 1) * half
                ].astype(F32)
    other = joined(dx[0, dx.shape[1] - 16 : dx.shape[1], :])
    bias_out[...] = jnp.where(x == y, total3[...], other)


def input_body(ny, pos, g, go, near, far, wt, out, buf):
    planes, cells, half = g.shape
    odd, y = pos[0], pos[1]

    def whole(p):
        mine, other = g[p], go[p]
        first = jnp.where(y == 0, mine, other)
        second = jnp.where(y == 0, other, mine)
        return jnp.concatenate([first, second], axis=1)

    for p in range(planes):
        put_plane(buf, p + 1, whole(p), ny, True)
    put_plane(buf, jnp.where(odd == 0, planes + 1, 0), near[...], ny, True)
    put_plane(buf, jnp.where(odd == 0, 0, planes + 1), far[...], ny, True)
    lanes = 2 * half
    for z in range(planes):
        acc = jnp.zeros((cells, out.shape[1]), F32)
        for a in range(3):
            for b in range(3):
                for c in range(3):
                    lhs = buf[z + 2 - a, (2 - b) * ny : (2 - b) * ny + cells, c * lanes : (c + 1) * lanes]
                    acc = acc + lax.dot_general(
                        lhs, wt[(a * 3 + b) * 3 + c], (((1,), (1,)), ((), ())), preferred_element_type=F32
                    )
        out[z * cells : (z + 1) * cells, :] = acc.astype(BF)


def per_device(volumes, weight, bias, cotangent):
    samples, planes, nx, ny, local_in = volumes.shape
    outputs = weight.shape[4]
    local_out = bias.shape[0]
    plane = nx * ny
    cells = planes * plane
    slabs = lax.axis_size("slab")
    s, z, y = lax.axis_index("slab"), lax.axis_index("dp"), lax.axis_index("chan")
    odd, mine, x = s % 2, s % 4, (s // 2) % 2
    pos = jnp.stack([odd, y, mine, odd, z % 2, (z // 2) % 2, x]).astype(jnp.int32)
    factor = float(samples * cells * slabs * lax.axis_size("dp")) ** -0.5

    def pair_edges(field):
        first, final = field[0], field[planes - 1]
        near = swap(jnp.where(odd == 0, final, first), "slab", 1)
        pairs = [(i, i + 1) for i in range(1, slabs - 1, 2)]
        far = lax.ppermute(jnp.where(odd == 0, first, final), "slab", pairs + [(j, i) for i, j in pairs])
        return near, far

    vol = volumes.reshape(planes, plane, local_in)
    near, far = pair_edges(vol)
    own, send = vmem_call(
        functools.partial(forward_body, ny),
        [((cells, local_out), F32), ((cells, local_out), BF)],
        [pltpu.VMEM((planes + 2, plane + 2 * ny, 3 * local_in), BF)],
        2 * cells * 27 * local_in * outputs,
        pos, vol, near, far, weight.reshape(3, 9 * local_in, outputs),
    )
    recv = swap(send, "chan", 1)
    vol_x = swap(vol, "slab", 2)
    vol_c = swap(jnp.concatenate([vol, vol_x], axis=0), "slab", 1)
    ends = group_ends(vol, slabs)
    vt = vmem_call(
        volume_body,
        [((4 * planes + 4, 3 * local_in // 2, plane), BF)],
        [],
        0,
        pos, vol, vol_x, vol_c, ends,
    )[0]

    act, grad = vmem_call(
        gate_body,
        [((cells, local_out), BF), ((cells, local_out), BF)],
        [],
        0,
        pos, own, recv, bias.reshape(1, local_out), cotangent.reshape(cells, local_out),
    )
    grad = grad.reshape(planes, plane, local_out)
    grad_y = swap(grad, "chan", 1)
    mine_x = jnp.where(x == y, grad, grad_y)
    g_x = swap(jnp.where(x == y, grad_y, grad), "slab", 2)
    g_c = swap(jnp.concatenate([mine_x, g_x], axis=0), "slab", 1)
    rows, lanes = 3 * local_in // 2, 3 * local_out
    keep1, send1, total1 = vmem_call(
        functools.partial(kernel_body, ny),
        [((3 * rows // 2, lanes), F32), ((3 * rows // 2 + 16, lanes), BF), ((8, local_out), F32)],
        [pltpu.VMEM((4 * planes, plane + 2 * ny, lanes), BF), pltpu.VMEM((rows, lanes), F32)],
        2 * cells * 27 * local_in * outputs,
        pos, vt, mine_x, g_x, g_c,
    )
    bit = 4
    while bit < slabs:
        keep1 = keep1 + swap(keep1, "slab", bit)
        total1 = total1 + swap(total1, "slab", bit)
        wide = send1[: 3 * rows // 2].astype(F32)
        wide = wide + swap(wide, "slab", bit)
        high = total1.astype(BF)
        mid = (total1 - high.astype(F32)).astype(BF)
        low = (total1 - high.astype(F32) - mid.astype(F32)).astype(BF)
        tail = jnp.tile(jnp.concatenate([high, mid, low], axis=1), (2, 1))
        send1 = jnp.concatenate([wide.astype(BF), tail], axis=0)
        bit *= 2
    recv1 = swap(send1, "dp", 1)
    keep2, send2, total2 = vmem_call(
        second_body,
        [((3 * rows // 4, lanes), F32), ((3 * rows // 4 + 16, lanes), BF), ((8, local_out), F32)],
        [],
        0,
        pos, keep1, recv1, total1,
    )
    recv2 = swap(send2, "dp", 2)
    quarter, total3 = vmem_call(
        functools.partial(last_body, factor),
        [((3 * rows // 4 + 16, lanes), BF), ((8, local_out), F32)],
        [],
        0,
        pos, keep2, recv2, total2,
    )
    q2 = swap(quarter, "dp", 2)
    q1 = swap(quarter, "dp", 1)
    q3 = swap(q2, "dp", 1)
    d = jnp.stack([quarter, q2, q1, q3])
    dx = swap(d, "slab", 2)
    e = swap(jnp.stack([d, dx]), "slab", 1)
    weight_grad, bias_grad = spread(pos, d, dx, e, total3, local_in, outputs)

    g_whole = jnp.concatenate([jnp.where(y == 0, grad, grad_y), jnp.where(y == 0, grad_y, grad)], axis=2)
    g_near, g_far = pair_edges(g_whole)
    input_grad = vmem_call(
        functools.partial(input_body, ny),
        [((cells, local_in), BF)],
        [pltpu.VMEM((planes + 2, plane + 2 * ny, 3 * outputs), BF)],
        2 * cells * 27 * local_in * outputs,
        pos, grad, grad_y, g_near, g_far, weight.reshape(27, local_in, outputs),
    )[0]
    shape = (samples, planes, nx, ny)
    return act.reshape(shape + (local_out,)), input_grad.reshape(shape + (local_in,)), weight_grad, bias_grad[0]


def group_ends(vol, slabs):
    before, after = jnp.zeros_like(vol[0]), jnp.zeros_like(vol[0])
    for group in range(4 if slabs > 4 else 0):
        up = [(i - 1, i + group) for i in range(4, slabs, 4)]
        down = [(i + 4, i + group) for i in range(0, slabs - 4, 4)]
        before = before + lax.ppermute(vol[vol.shape[0] - 1], "slab", up)
        after = after + lax.ppermute(vol[0], "slab", down)
    return jnp.stack([before, after])


def spread(pos, d, dx, e, total3, local_in, outputs):
    whole = pl.BlockSpec(memory_space=pltpu.VMEM)
    return pl.pallas_call(
        spread_body,
        grid=(3, 3),
        out_shape=[
            jax.ShapeDtypeStruct((3, 3, 3, local_in, outputs), F32),
            jax.ShapeDtypeStruct(total3.shape, F32),
        ],
        in_specs=[pl.BlockSpec(memory_space=pltpu.SMEM), whole, whole, whole, whole],
        out_specs=[
            pl.BlockSpec((1, 1, 3, local_in, outputs), lambda i, j: (i, j, 0, 0, 0)),
            pl.BlockSpec(total3.shape, lambda i, j: (0, 0)),
        ],
        compiler_params=pltpu.CompilerParams(vmem_limit_bytes=20 * MIB),
    )(pos, d, dx, e, total3)


def solution(mesh):
    placed = (
        P("dp", "slab", None, None, "chan"),
        P(None, None, None, "chan", None),
        P("chan"),
        P("dp", "slab", None, None, "chan"),
    )
    return jax.shard_map(
        per_device,
        mesh=mesh,
        in_specs=placed,
        out_specs=(
            P("dp", "slab", None, None, "chan"),
            P("dp", "slab", None, None, "chan"),
            P(None, None, None, "chan", None),
            P("chan"),
        ),
        check_vma=False,
    )
```

```python
import functools

import jax
import jax.numpy as jnp
from jax import lax
from jax.experimental import pallas as pl
from jax.experimental.pallas import tpu as pltpu
from jax.sharding import PartitionSpec as P

BF = jnp.bfloat16
F32 = jnp.float32
MIB = 1 << 20


def swap(value, axis, bit):
    return lax.ppermute(value, axis, [(i, i ^ bit) for i in range(lax.axis_size(axis))])


def vmem_call(body, outs, scratch, flops, *args, left=(), after=(), limit=20):
    shapes = [jax.ShapeDtypeStruct(s, d) for s, d in outs]
    count, waited = len(args), len(after)

    def inner(*refs):
        body(*refs[:count], *refs[count + waited :])

    specs = [pl.BlockSpec(memory_space=pl.ANY if n in left else pltpu.VMEM) for n in range(1, count)]
    return pl.pallas_call(
        inner,
        out_shape=shapes,
        in_specs=[pl.BlockSpec(memory_space=pltpu.SMEM)] + specs + [pl.BlockSpec(memory_space=pl.ANY)] * waited,
        out_specs=[pl.BlockSpec(memory_space=pltpu.VMEM)] * len(shapes),
        scratch_shapes=scratch,
        compiler_params=pltpu.CompilerParams(vmem_limit_bytes=limit * MIB),
        cost_estimate=pl.CostEstimate(flops=4 * flops + 10**9, bytes_accessed=MIB, transcendentals=0),
    )(*args, *after)


def shift_y(value, step, ny):
    rows = value.shape[0]
    y = lax.broadcasted_iota(jnp.int32, value.shape, 0) % ny
    rolled = pltpu.roll(value, (-step) % rows, 0)
    return jnp.where(y == (0 if step < 0 else ny - 1), 0.0, rolled)


def put_plane(buf, at, value, ny, flip):
    cells, lanes = value.shape
    wide = value.astype(F32)
    edge = jnp.zeros((ny, 3 * lanes), BF)
    buf[at, 0:ny, :] = edge
    buf[at, ny + cells : 2 * ny + cells, :] = edge
    for c in range(3):
        step = (1 - c) if flip else (c - 1)
        moved = value if step == 0 else shift_y(wide, step, ny).astype(BF)
        buf[at, ny : ny + cells, c * lanes : (c + 1) * lanes] = moved


def near_body(ny, pos, plane, vol_n, vol_f, w, own, send, kept, held, buf, sem):
    copy = pltpu.make_async_copy(w, held, sem)
    copy.start()
    put_plane(kept, 0, vol_n[...], ny, False)
    put_plane(kept, 1, vol_f[...], ny, False)
    outer_body(ny, pos, plane, kept, w, own, send, buf)
    copy.wait()


def outer_body(ny, pos, plane, kept, w, own, send, buf):
    cells = plane.shape[0]
    y, depth, at = pos[1], pos[7], pos[8]
    half = own.shape[1]
    put_plane(buf, 0, plane[...], ny, False)
    total = tap(kept.at[at], w, 1, ny, cells) + tap(kept.at[1 - at], w, 2 - depth, ny, cells)
    total = total + tap(buf.at[0], w, depth, ny, cells)
    own[...] = jnp.where(y == 0, total[:, :half], total[:, half:])
    send[...] = jnp.where(y == 0, total[:, half:], total[:, :half]).astype(BF)


def tap(field, w, depth, ny, cells):
    lhs = jnp.concatenate([field[b * ny : b * ny + cells, :] for b in range(3)], axis=1)
    return jnp.dot(lhs, w[depth], preferred_element_type=F32)


def gate(pos, plane, own, recv, bias, cot):
    pre = own[...] + recv[...].astype(F32) + bias[...].astype(F32)
    s = 1.0 / (1.0 + jnp.exp(-pre))
    return (pre * s).astype(BF), (cot[plane].astype(F32) * s * (1.0 + pre * (1.0 - s))).astype(BF)


def near_gate_body(pos, own, recv, bias, cot, act, grad):
    act[...], grad[...] = gate(pos, 1 - pos[0], own, recv, bias, cot)


def far_gate_body(pos, own, recv, bias, cot, act, grad):
    act[...], grad[...] = gate(pos, pos[0], own, recv, bias, cot)


def pack_body(pos, *refs):
    out, at = refs[-1], 0
    for ref in refs[:-1]:
        if len(ref.shape) == 3:
            for n in range(ref.shape[0]):
                out[at + n] = ref[n]
            at += ref.shape[0]
        else:
            out[at] = ref[...]
            at += 1


def pack(pos, *arrays, after=()):
    count = sum(a.shape[0] if a.ndim == 3 else 1 for a in arrays)
    return vmem_call(
        pack_body, [((count,) + arrays[0].shape[-2:], arrays[0].dtype)], [], 0, pos, *arrays, after=after
    )[0]


def volume_body(pos, v0, v1, v2, v3, ends, vt):
    planes, cells, lanes = v0.shape
    mine, k = pos[2], pos[3]
    keep = lanes // 2

    def put(at, value):
        turned = value.astype(F32).T
        turned = jnp.where(k == 0, turned[:keep], turned[keep:]).astype(BF)
        for a in range(3):
            vt[at + 2 - a, a * keep : (a + 1) * keep, :] = turned

    put(0, ends[0])
    put(4 * planes + 1, ends[1])
    for p in range(planes):
        for who, field in enumerate((v0, v1, v2, v3)):
            put((mine ^ who) * planes + p + 1, field[p])


def kernel_terms(ny, pos, near, vt, grads, buf, acc, before):
    cells, lanes = grads[0][1].shape
    mine, odd = pos[2], pos[0]
    bsum = jnp.zeros((1, lanes), F32)
    where = []
    for n, (who, ref) in enumerate(grads):
        own_odd = odd if who in (0, 2) else 1 - odd
        where.append((mine ^ who) * 2 + (1 - own_odd if near else own_odd) + 2)
        value = ref[...]
        put_plane(buf, n, value, ny, True)
        bsum = bsum + jnp.sum(value.astype(F32), axis=0, keepdims=True)
    lhs = jnp.concatenate([vt[at] for at in where], axis=1)
    for b in range(3):
        rhs = jnp.concatenate(
            [buf[n, (2 - b) * ny : (2 - b) * ny + cells, :] for n in range(len(grads))], axis=0
        )
        summed = jnp.dot(lhs, rhs, preferred_element_type=F32)
        acc[b] = summed if before is None else summed + before[b]
    return bsum


def near_kernel_body(ny, pos, vt, g0, g1, g2, g3, keep_f, acc, total, sent, buf):
    sent[...] = keep_f[...]
    bsum = kernel_terms(ny, pos, True, vt, ((0, g0), (1, g1), (2, g2), (3, g3)), buf, acc, None)
    total[...] = jnp.broadcast_to(bsum, total.shape)


def mid_kernel_body(ny, pos, vt, g0, g2, acc0, total0, acc, total, buf):
    bsum = kernel_terms(ny, pos, False, vt, ((0, g0), (2, g2)), buf, acc, acc0)
    total[...] = total0[...] + jnp.broadcast_to(bsum, total.shape)


def far_kernel_body(ny, pos, vt, g1, g3, acc0, total0, acc, total, buf):
    bsum = kernel_terms(ny, pos, False, vt, ((1, g1), (3, g3)), buf, acc, acc0)
    total[...] = total0[...] + jnp.broadcast_to(bsum, total.shape)


def last_kernel_body(ny, pos, vt, g1, g3, acc0, total0, keep, s1, s2, s3, total, buf, acc):
    far_kernel_body(ny, pos, vt, g1, g3, acc0, total0, acc, total, buf)
    cut_body(pos, acc, total, keep, s1, s2, s3)


def cut_body(pos, acc, total, keep, s1, s2, s3):
    part = keep.shape[0] // 9
    mine = pos[4]
    for b in range(3):
        for a in range(3):
            rows = slice((3 * b + a) * part, (3 * b + a + 1) * part)
            keep[rows, :] = acc[b, pl.ds(pl.multiple_of((4 * a + mine) * part, part), part), :]
            for who, ref in ((1, s1), (2, s2), (3, s3)):
                at = pl.multiple_of((4 * a + (mine ^ who)) * part, part)
                ref[rows, :] = acc[b, pl.ds(at, part), :].astype(BF)
    for ref in (s1, s2, s3):
        ref[9 * part : 9 * part + 16, :] = split_rows(total)


def split_rows(total):
    value = jnp.broadcast_to(total[0:1, :], (16, total.shape[1]))
    high = value.astype(BF)
    rest = value - high.astype(F32)
    mid = rest.astype(BF)
    low = (rest - mid.astype(F32)).astype(BF)
    return jnp.concatenate([high, mid, low], axis=1)


def joined(rows):
    n = rows.shape[1] // 3
    wide = rows[0:8, :].astype(F32)
    return wide[:, :n] + wide[:, n : 2 * n] + wide[:, 2 * n :]


def sum_body(factor, pos, keep, r1, r2, r3, total, quarter, quarter_b, total3):
    rows = keep.shape[0]
    tails = [joined(ref[rows : rows + 16, :]) for ref in (r1, r2, r3)]
    total3[...] = ((total[...] + tails[0]) + (tails[1] + tails[2])) * factor
    one = keep[...] + r1[0:rows, :].astype(F32)
    two = r2[0:rows, :].astype(F32) + r3[0:rows, :].astype(F32)
    quarter[...] = ((one + two) * factor).astype(BF)
    quarter_b[0:rows, :] = quarter[...]
    quarter_b[rows : rows + 16, :] = split_rows(total3)


def place(pos, pieces, out, wide, sems):
    x, k, mine = pos[6], pos[3], pos[4]
    half = out.shape[2] // 2
    copies = []
    for n, (who, j, piece) in enumerate(pieces):
        for b in range(3):
            for a in range(3):
                for c in range(3):
                    rows = slice((3 * b + a) * 16, (3 * b + a + 1) * 16)
                    wide[n, (a * 3 + b) * 3 + c] = piece[rows, c * half : (c + 1) * half].astype(F32)
        row = pl.multiple_of((k ^ (who >> 1)) * 64 + (mine ^ j) * 16, 16)
        lane = pl.multiple_of((x ^ (who & 1)) * half, half)
        copy = pltpu.make_async_copy(wide.at[n], out.at[:, pl.ds(row, 16), pl.ds(lane, half)], sems.at[n])
        copy.start()
        copies.append(copy)
    for copy in copies:
        copy.wait()


def round_body(pos, q, q1, q2, x0, one_z, two_x, four_c):
    one_z[...] = q2[...]
    two_x[0], two_x[1] = q1[...], q2[...]
    four_c[0], four_c[1], four_c[2], four_c[3] = q[...], q1[...], q2[...], x0[0 : q.shape[0], :]


def next_round_body(pos, q3, x12, one_x, three_c):
    one_x[...] = q3[...]
    three_c[0], three_c[1], three_c[2] = q3[...], x12[0], x12[1]


def first_spread_body(pos, own, core, out, done, wide, sems):
    kinds = ((0, 0), (0, 1), (0, 2), (1, 0))
    pieces = [(who, j, own.at[n]) for n, (who, j) in enumerate(kinds)]
    pieces += [(who + 2, j, core.at[n]) for n, (who, j) in enumerate(kinds)]
    place(pos, pieces, out, wide, sems)
    done[...] = jnp.zeros_like(done)


def next_spread_body(pos, own, core, before, out, done, wide, sems):
    kinds = ((0, 3), (1, 1), (1, 2))
    pieces = [(who, j, own.at[n]) for n, (who, j) in enumerate(kinds)]
    pieces += [(who + 2, j, core.at[n]) for n, (who, j) in enumerate(kinds)]
    place(pos, pieces, out, wide, sems)
    done[...] = jnp.zeros_like(done)


def last_spread_body(pos, x0, x3, core3, total3, before, out, bias_out, wide, sems):
    place(pos, [(1, 3, x3), (3, 3, core3)], out, wide, sems)
    rows = x3.shape[0]
    other = joined(x0[rows : rows + 16, :])[0:1, :]
    bias_out[...] = jnp.where(pos[6] == pos[1], total3[0:1, :], other)


def spread(body, shape, small, after, pos, *arrays, alias=False):
    whole = pl.BlockSpec(memory_space=pltpu.VMEM)
    anywhere = pl.BlockSpec(memory_space=pl.ANY)
    count, waited = 1 + len(arrays), len(after)

    def inner(*refs):
        body(*refs[:count], *refs[count + waited :])

    specs = [pl.BlockSpec(memory_space=pltpu.SMEM)] + [whole] * (len(arrays) - alias) + [anywhere] * alias
    return pl.pallas_call(
        inner,
        out_shape=[jax.ShapeDtypeStruct(shape, F32), jax.ShapeDtypeStruct(*small)],
        in_specs=specs + [anywhere] * waited,
        out_specs=[anywhere, whole],
        scratch_shapes=[pltpu.VMEM((8, shape[0], 16, shape[2] // 2), F32), pltpu.SemaphoreType.DMA((8,))],
        input_output_aliases={count - 1: 0} if alias else {},
        compiler_params=pltpu.CompilerParams(vmem_limit_bytes=20 * MIB),
        cost_estimate=pl.CostEstimate(flops=1, bytes_accessed=1, transcendentals=0),
    )(pos, *arrays, *after)


def whole(x, keep, other):
    first = jnp.where(x == 0, keep, other)
    return jnp.concatenate([first, jnp.where(x == 0, other, keep)], axis=1)


def input_taps(ny, fields, depths, wt, cells, buf, out_rows):
    lanes = buf.shape[2] // 3
    for n, field in enumerate(fields):
        put_plane(buf, n, field, ny, True)
    acc = jnp.zeros((cells, wt.shape[1]), F32)
    for n, depth in enumerate(depths):
        for b in range(3):
            for c in range(3):
                lhs = buf[n, (2 - b) * ny : (2 - b) * ny + cells, c * lanes : (c + 1) * lanes]
                acc = acc + lax.dot_general(
                    lhs, wt[depth * 9 + b * 3 + c], (((1,), (1,)), ((), ())), preferred_element_type=F32
                )
    return acc.astype(BF)


def near_input_body(ny, pos, kn, on, kf, of, near, near_o, wt, act_n, act_f, out, act, buf):
    odd, x = pos[0], pos[6]
    fields = (whole(x, kf[...], of[...]), whole(x, kn[...], on[...]), whole(x, near[...], near_o[...]))
    out[...] = input_taps(ny, fields, (2 - 2 * odd, 1, 2 * odd), wt, kn.shape[0], buf, out)
    act[1 - odd] = act_n[...]
    act[odd] = act_f[...]


def far_input_body(inside, ny, pos, kn, on, kf, of, far, far_o, wt, ig_n, out, done, buf):
    odd, x, mine = pos[0], pos[6], pos[2]
    beyond = far[...]
    if inside:
        beyond = jnp.where((mine == 0) | (mine == 3), jnp.zeros_like(beyond), beyond)
    fields = (whole(x, kn[...], on[...]), whole(x, kf[...], of[...]), whole(x, beyond, far_o[...]))
    out[odd] = input_taps(ny, fields, (2 * odd, 1, 2 - 2 * odd), wt, kn.shape[0], buf, out)
    out[1 - odd] = ig_n[...]
    done[...] = jnp.zeros_like(done)


def per_device(volumes, weight, bias, cotangent):
    samples, planes, nx, ny, local_in = volumes.shape
    outputs = weight.shape[4]
    local_out = bias.shape[0]
    plane = nx * ny
    cells = planes * plane
    slabs = lax.axis_size("slab")
    s, z, y = lax.axis_index("slab"), lax.axis_index("dp"), lax.axis_index("chan")
    odd, mine, x = s % 2, s % 4, (s // 2) % 2
    near_depth, far_depth = 2 - 2 * odd, 2 * odd
    pos = jnp.stack([odd, y, mine, odd, z, z, x, near_depth, 0 * x]).astype(jnp.int32)
    pos_far = jnp.stack([odd, y, mine, odd, z, z, x, far_depth, 0 * x + 1]).astype(jnp.int32)
    factor = float(samples * cells * slabs * lax.axis_size("dp")) ** -0.5
    padded = plane + 2 * ny
    macs = plane * 27 * local_in * outputs

    def next_pair(value):
        pairs = [(i, i + 1) for i in range(1, slabs - 1, 2)]
        return lax.ppermute(value, "slab", pairs + [(j, i) for i, j in pairs])

    vol = volumes.reshape(planes, plane, local_in)
    w = weight.reshape(3, 9 * local_in, outputs)
    vol_n = jnp.where(odd == 0, vol[1], vol[0])
    vol_f = jnp.where(odd == 0, vol[0], vol[1])
    near, far = swap(vol_n, "slab", 1), next_pair(vol_f)
    ends = group_ends(vol, slabs)
    wide, thin = ((plane, local_out), F32), ((plane, local_out), BF)
    one = [pltpu.VMEM((1, padded, 3 * local_in), BF)]
    own_n, send_n, kept, held = vmem_call(
        functools.partial(near_body, ny),
        [wide, thin, ((2, padded, 3 * local_in), BF), (w.shape, BF)],
        one + [pltpu.SemaphoreType.DMA(())],
        macs,
        pos, near, vol_n, vol_f, w,
    )
    recv_n = swap(send_n, "chan", 1)
    own_f, send_f = vmem_call(functools.partial(outer_body, ny), [wide, thin], one, macs, pos_far, far, kept, held)
    recv_f = swap(send_f, "chan", 1)
    vol_x = swap(vol, "slab", 2)
    vol_c, vol_cx = swap(vol, "slab", 1), swap(vol_x, "slab", 1)

    bias_row, cot = bias.reshape(1, local_out), cotangent.reshape(planes, plane, local_out)
    act_n, g_n = vmem_call(near_gate_body, [thin, thin], [], 0, pos, own_n, recv_n, bias_row, cot)
    g_ny = swap(g_n, "chan", 1)
    act_f, g_f = vmem_call(far_gate_body, [thin, thin], [], 0, pos, own_f, recv_f, bias_row, cot, after=(g_n,))
    g_fy = swap(g_f, "chan", 1)
    lanes = 3 * local_out

    def routed(mine_g, other_g):
        keep, send = jnp.where(x == y, mine_g, other_g), jnp.where(x == y, other_g, mine_g)
        return keep, send, swap(send, "slab", 2)

    keep_n, send_n, got_n = routed(g_n, g_ny)
    core_n = swap(keep_n, "slab", 1), swap(got_n, "slab", 1)
    keep_f, send_f, got_f = routed(g_f, g_fy)
    vt = vmem_call(
        volume_body,
        [((4 * planes + 4, 3 * local_in // 2, plane), BF)],
        [],
        0,
        pos, vol, vol_c, vol_x, vol_cx, ends,
        after=(g_f,),
    )[0]
    acc_shape = (3, 3 * local_in // 2, lanes)
    buf = pltpu.VMEM((4, padded, lanes), BF)
    acc0, total0, sent = vmem_call(
        functools.partial(near_kernel_body, ny),
        [(acc_shape, F32), ((8, local_out), F32), thin],
        [buf],
        2 * macs,
        pos, vt, keep_n, core_n[0], got_n, core_n[1], keep_f,
    )
    core_f = swap(keep_f, "slab", 1), swap(pack(pos, got_f, after=(acc0,))[0], "slab", 1)
    pair = pltpu.VMEM((2, padded, lanes), BF)
    sums = [(acc_shape, F32), ((8, local_out), F32)]
    acc1, total1 = vmem_call(
        functools.partial(mid_kernel_body, ny), sums, [pair], macs, pos, vt, keep_f, got_f, acc0, total0
    )
    rows = 9 * local_in // 8
    cut = [((rows, lanes), F32)] + [((rows + 16, lanes), BF)] * 3
    if slabs == 4:
        keep, s1, s2, s3, total = vmem_call(
            functools.partial(last_kernel_body, ny),
            cut + [((8, local_out), F32)],
            [pair, pltpu.VMEM(acc_shape, F32)],
            macs,
            pos, vt, *core_f, acc1, total1,
        )
    else:
        acc, total = vmem_call(
            functools.partial(far_kernel_body, ny), sums, [pair], macs, pos, vt, *core_f, acc1, total1
        )
        bit = 4
        while bit < slabs:
            acc, total = acc + swap(acc, "slab", bit), total + swap(total, "slab", bit)
            bit *= 2
        keep, s1, s2, s3 = vmem_call(cut_body, cut, [], 0, pos, acc, total)
    r1, r2, r3 = swap(s1, "dp", 1), swap(s2, "dp", 2), swap(s3, "dp", 3)

    wt = weight.reshape(27, local_in, outputs)
    ig_buf = pltpu.VMEM((3, padded, 3 * outputs), BF)
    ig_n, act = vmem_call(
        functools.partial(near_input_body, ny),
        [((plane, local_in), BF), ((planes, plane, local_out), BF)],
        [ig_buf],
        2 * macs,
        pos, keep_n, send_n, keep_f, send_f, core_n[0], swap(send_n, "slab", 1), wt, act_n, act_f,
        after=(s1,),
    )
    far_keep = core_f[1]
    if slabs > 4:
        far_keep = jnp.where((mine == 0) | (mine == 3), next_pair(send_f), far_keep)
    ig, ig_done = vmem_call(
        functools.partial(far_input_body, slabs == 4, ny),
        [((planes, plane, local_in), BF), ((8, 128), F32)],
        [ig_buf],
        2 * macs,
        pos, keep_n, send_n, keep_f, send_f, far_keep, next_pair(sent), wt, ig_n,
        after=(s1,),
    )
    quarter, quarter_b, total3 = vmem_call(
        functools.partial(sum_body, factor),
        [((rows, lanes), BF), ((rows + 16, lanes), BF), ((8, local_out), F32)],
        [],
        0,
        pos, keep, r1, r2, r3, total,
        after=(ig_done,),
    )
    q1, q2, x0 = swap(quarter, "dp", 1), swap(quarter, "dp", 2), swap(quarter_b, "slab", 2)
    one_z, two_x, four_c = vmem_call(
        round_body,
        [(quarter.shape, BF), ((2,) + quarter.shape, BF), ((4,) + quarter.shape, BF)],
        [],
        0,
        pos, quarter, q1, q2, x0,
    )
    q3, x12, core = swap(one_z, "dp", 1), swap(two_x, "slab", 2), swap(four_c, "slab", 1)
    one_x, three_c = vmem_call(
        next_round_body, [(quarter.shape, BF), ((3,) + quarter.shape, BF)], [], 0, pos, q3, x12, after=(core,)
    )
    x3, core_b = swap(one_x, "slab", 2), swap(three_c, "slab", 1)
    out_shape = (27, local_in, outputs)
    token = (8, 128), F32
    out, _ = spread(first_spread_body, out_shape, token, (one_x,), pos, four_c, core)
    out, done = spread(next_spread_body, out_shape, token, (), pos, three_c, core_b, out, alias=True)
    core_x3 = swap(pack(pos, x3, after=(done,))[0], "slab", 1)
    last = (1, local_out), F32
    weight_grad, bias_grad = spread(
        last_spread_body, out_shape, last, (), pos, x0, x3, core_x3, total3, out, alias=True
    )
    shape = (samples, planes, nx, ny)
    return (
        act.reshape(shape + (local_out,)),
        ig.reshape(shape + (local_in,)),
        weight_grad.reshape(weight.shape),
        bias_grad[0],
    )


def group_ends(vol, slabs):
    before, after = jnp.zeros_like(vol[0]), jnp.zeros_like(vol[0])
    for group in range(4 if slabs > 4 else 0):
        up = [(i - 1, i + group) for i in range(4, slabs, 4)]
        down = [(i + 4, i + group) for i in range(0, slabs - 4, 4)]
        before = before + lax.ppermute(vol[vol.shape[0] - 1], "slab", up)
        after = after + lax.ppermute(vol[0], "slab", down)
    return jnp.stack([before, after])


def solution(mesh):
    placed = (
        P("dp", "slab", None, None, "chan"),
        P(None, None, None, "chan", None),
        P("chan"),
        P("dp", "slab", None, None, "chan"),
    )
    return jax.shard_map(
        per_device,
        mesh=mesh,
        in_specs=placed,
        out_specs=(
            P("dp", "slab", None, None, "chan"),
            P("dp", "slab", None, None, "chan"),
            P(None, None, None, "chan", None),
            P("chan"),
        ),
        check_vma=False,
    )
```

```python
import functools

import jax
import jax.numpy as jnp
from jax import lax
from jax.experimental import pallas as pl
from jax.experimental.pallas import tpu as pltpu
from jax.sharding import PartitionSpec as P

BF = jnp.bfloat16
F32 = jnp.float32
MIB = 1 << 20


def swap(value, axis, bit):
    return lax.ppermute(value, axis, [(i, i ^ bit) for i in range(lax.axis_size(axis))])


def vmem_call(body, outs, scratch, flops, *args, left=(), after=(), limit=20):
    shapes = [jax.ShapeDtypeStruct(s, d) for s, d in outs]
    count, waited = len(args), len(after)

    def inner(*refs):
        body(*refs[:count], *refs[count + waited :])

    specs = [pl.BlockSpec(memory_space=pl.ANY if n in left else pltpu.VMEM) for n in range(1, count)]
    return pl.pallas_call(
        inner,
        out_shape=shapes,
        in_specs=[pl.BlockSpec(memory_space=pltpu.SMEM)] + specs + [pl.BlockSpec(memory_space=pl.ANY)] * waited,
        out_specs=[pl.BlockSpec(memory_space=pltpu.VMEM)] * len(shapes),
        scratch_shapes=scratch,
        compiler_params=pltpu.CompilerParams(vmem_limit_bytes=limit * MIB),
        cost_estimate=pl.CostEstimate(flops=4 * flops + 10**9, bytes_accessed=MIB, transcendentals=0),
    )(*args, *after)


def shift_y(value, step, ny):
    rows = value.shape[0]
    y = lax.broadcasted_iota(jnp.int32, value.shape, 0) % ny
    rolled = pltpu.roll(value, (-step) % rows, 0)
    return jnp.where(y == (0 if step < 0 else ny - 1), 0.0, rolled)


def put_plane(buf, at, value, ny, flip):
    cells, lanes = value.shape
    wide = value.astype(F32)
    edge = jnp.zeros((ny, 3 * lanes), BF)
    buf[at, 0:ny, :] = edge
    buf[at, ny + cells : 2 * ny + cells, :] = edge
    for c in range(3):
        step = (1 - c) if flip else (c - 1)
        moved = value if step == 0 else shift_y(wide, step, ny).astype(BF)
        buf[at, ny : ny + cells, c * lanes : (c + 1) * lanes] = moved


def near_body(ny, pos, vol_n, vol_f, plane, w, own, send, kept, held, done, buf, sem):
    copy = pltpu.make_async_copy(w, held, sem)
    copy.start()
    put_plane(kept, 0, vol_n[...], ny, False)
    put_plane(kept, 1, vol_f[...], ny, False)
    put_plane(buf, 0, plane[...], ny, False)
    sums(ny, pos, kept.at[0], kept.at[1], buf.at[0], 2 - 2 * pos[0], w, own, send)
    done[...] = jnp.zeros_like(done)
    copy.wait()


def far_body(ny, pos, beyond, kept, w, own, send, buf):
    odd = pos[0]
    put_plane(buf, 0, jnp.where(pos[7] == 0, 0.0, beyond[...].astype(F32)).astype(BF), ny, False)
    sums(ny, pos, kept.at[1], kept.at[0], buf.at[0], 2 * odd, w, own, send)


def sums(ny, pos, middle, inner, outer, depth, w, own, send):
    cells = own.shape[0]
    y, half = pos[1], own.shape[1]
    total = tap(middle, w, 1, ny, cells) + tap(inner, w, 2 - depth, ny, cells) + tap(outer, w, depth, ny, cells)
    own[...] = jnp.where(y == 0, total[:, :half], total[:, half:])
    send[...] = jnp.where(y == 0, total[:, half:], total[:, :half]).astype(BF)


def tap(field, w, depth, ny, cells):
    lhs = jnp.concatenate([field[b * ny : b * ny + cells, :] for b in range(3)], axis=1)
    return jnp.dot(lhs, w[depth], preferred_element_type=F32)


def gate(pos, plane, own, recv, bias, cot):
    pre = own[...] + recv[...].astype(F32) + bias[...].astype(F32)
    s = 1.0 / (1.0 + jnp.exp(-pre))
    return (pre * s).astype(BF), (cot[plane].astype(F32) * s * (1.0 + pre * (1.0 - s))).astype(BF)


def near_gate_body(pos, own, recv, bias, cot, vol_n, act, grad, vol_out):
    act[...], grad[...] = gate(pos, 1 - pos[0], own, recv, bias, cot)
    vol_out[...] = vol_n[...]


def far_gate_body(pos, own, recv, bias, cot, act, grad):
    act[...], grad[...] = gate(pos, pos[0], own, recv, bias, cot)


def held_back(value, *tokens):
    rows, lanes = value.shape
    ready = functools.reduce(jnp.logical_and, [token == token for token in tokens])
    blocks = value.reshape(rows // 8, 8, lanes)
    return jnp.where(ready[None], blocks, jnp.zeros_like(blocks)).reshape(rows, lanes)


def volume_body(pos, n0, f0, n1, f1, n2, f2, n3, f3, ends, vt):
    lanes = n0.shape[1]
    mine, k, odd = pos[2], pos[3], pos[0]
    keep = lanes // 2

    def put(at, value):
        turned = value.astype(F32).T
        turned = jnp.where(k == 0, turned[:keep], turned[keep:]).astype(BF)
        for a in range(3):
            vt[at + 2 - a, a * keep : (a + 1) * keep, :] = turned

    put(0, ends[0])
    put(9, ends[1])
    for who, (near, far) in enumerate(((n0, f0), (n1, f1), (n2, f2), (n3, f3))):
        own_odd = odd if who in (0, 2) else 1 - odd
        put((mine ^ who) * 2 + (1 - own_odd) + 1, near[...])
        put((mine ^ who) * 2 + own_odd + 1, far[...])


def kernel_terms(ny, pos, vt, grads, buf, acc, before):
    cells, lanes = grads[0][2].shape
    mine, odd = pos[2], pos[0]
    bsum = jnp.zeros((1, lanes), F32)
    where = []
    for n, (far, who, ref) in enumerate(grads):
        own_odd = odd if who in (0, 2) else 1 - odd
        where.append((mine ^ who) * 2 + (own_odd if far else 1 - own_odd) + 2)
        value = ref[...]
        put_plane(buf, n, value, ny, True)
        bsum = bsum + jnp.sum(value.astype(F32), axis=0, keepdims=True)
    lhs = jnp.concatenate([vt[at] for at in where], axis=1)
    for b in range(3):
        rhs = [buf[n, (2 - b) * ny : (2 - b) * ny + cells, :] for n in range(len(grads))]
        summed = jnp.dot(lhs, jnp.concatenate(rhs, axis=0), preferred_element_type=F32)
        acc[b] = summed if before is None else summed + before[b]
    return bsum


def first_kernel_body(ny, pos, vt, g0, g1, f0, f1, acc, total, buf):
    grads = ((0, 0, g0), (0, 1, g1), (1, 0, f0), (1, 1, f1))
    bsum = kernel_terms(ny, pos, vt, grads, buf, acc, None)
    total[...] = jnp.broadcast_to(jnp.concatenate([bsum] * 3, axis=1), total.shape)


def second_kernel_body(ny, pos, vt, g2, g3, acc0, total0, acc, total, buf):
    bsum = kernel_terms(ny, pos, vt, ((0, 2, g2), (0, 3, g3)), buf, acc, acc0)
    total[...] = total0[...] + jnp.concatenate([bsum] * 3, axis=1)


def next_kernel_body(who, ny, pos, vt, f, acc0, total0, acc, total, buf):
    bsum = kernel_terms(ny, pos, vt, ((1, who, f),), buf, acc, acc0)
    total[...] = total0[...] + jnp.concatenate([bsum] * 3, axis=1)


def last_kernel_body(ny, pos, vt, f3, acc0, total0, kf, keep, s1, s2, s3, total, sent, buf, acc):
    sent[...] = kf[...]
    next_kernel_body(3, ny, pos, vt, f3, acc0, total0, acc, total, buf)
    cut_body(pos, acc, keep, s1, s2, s3)


def cut_body(pos, acc, keep, s1, s2, s3):
    part = keep.shape[0] // 9
    mine = pos[4]
    for b in range(3):
        for a in range(3):
            rows = slice((3 * b + a) * part, (3 * b + a + 1) * part)
            for who, ref in ((0, keep), (1, s1), (2, s2), (3, s3)):
                at = pl.multiple_of((4 * a + (mine ^ who)) * part, part)
                ref[rows, :] = acc[b, pl.ds(at, part), :].astype(ref.dtype)


def place(pos, pieces, out, wide, sems):
    x, k, mine = pos[6], pos[3], pos[4]
    half = out.shape[2] // 2
    copies = []
    for n, (who, j, piece) in enumerate(pieces):
        for b in range(3):
            for a in range(3):
                for c in range(3):
                    rows = slice((3 * b + a) * 16, (3 * b + a + 1) * 16)
                    wide[n, (a * 3 + b) * 3 + c] = piece[rows, c * half : (c + 1) * half].astype(F32)
        row = pl.multiple_of((k ^ (who >> 1)) * 64 + (mine ^ j) * 16, 16)
        lane = pl.multiple_of((x ^ (who & 1)) * half, half)
        copy = pltpu.make_async_copy(wide.at[n], out.at[:, pl.ds(row, 16), pl.ds(lane, half)], sems.at[n])
        copy.start()
        copies.append(copy)
    for copy in copies:
        copy.wait()


def round_body(pos, q, q1, x0, q2, one_z, two_x, four_c):
    one_z[...] = q2[...]
    two_x[0], two_x[1] = q1[...], q2[...]
    four_c[0], four_c[1], four_c[2], four_c[3] = q[...], q1[...], q2[...], x0[...]


def next_round_body(pos, q3, x12, one_x, three_c):
    one_x[...] = q3[...]
    three_c[0], three_c[1], three_c[2] = q3[...], x12[0], x12[1]


def first_spread_body(pos, own, core, out, done, wide, sems):
    kinds = ((0, 0), (0, 1), (0, 2), (1, 0))
    pieces = [(who, j, own.at[n]) for n, (who, j) in enumerate(kinds)]
    pieces += [(who + 2, j, core.at[n]) for n, (who, j) in enumerate(kinds)]
    place(pos, pieces, out, wide, sems)
    done[...] = jnp.zeros_like(done)


def next_spread_body(pos, own, core, before, out, done, wide, sems):
    kinds = ((0, 3), (1, 1), (1, 2))
    pieces = [(who, j, own.at[n]) for n, (who, j) in enumerate(kinds)]
    pieces += [(who + 2, j, core.at[n]) for n, (who, j) in enumerate(kinds)]
    place(pos, pieces, out, wide, sems)
    done[...] = jnp.zeros_like(done)


def last_spread_body(pos, x3, cx3, before, out, done, wide, sems):
    place(pos, [(1, 3, x3), (3, 3, cx3)], out, wide, sems)
    done[...] = jnp.zeros_like(done)


def spread(body, shape, small, after, pos, *arrays, alias=False):
    whole = pl.BlockSpec(memory_space=pltpu.VMEM)
    anywhere = pl.BlockSpec(memory_space=pl.ANY)
    count, waited = 1 + len(arrays), len(after)

    def inner(*refs):
        body(*refs[:count], *refs[count + waited :])

    specs = [pl.BlockSpec(memory_space=pltpu.SMEM)] + [whole] * (len(arrays) - alias) + [anywhere] * alias
    return pl.pallas_call(
        inner,
        out_shape=[jax.ShapeDtypeStruct(shape, F32), jax.ShapeDtypeStruct(*small)],
        in_specs=specs + [anywhere] * waited,
        out_specs=[anywhere, whole],
        scratch_shapes=[pltpu.VMEM((8, shape[0], 16, shape[2] // 2), F32), pltpu.SemaphoreType.DMA((8,))],
        input_output_aliases={count - 1: 0} if alias else {},
        compiler_params=pltpu.CompilerParams(vmem_limit_bytes=20 * MIB),
        cost_estimate=pl.CostEstimate(flops=1, bytes_accessed=1, transcendentals=0),
    )(pos, *arrays, *after)


def whole(x, keep, other):
    first = jnp.where(x == 0, keep, other)
    return jnp.concatenate([first, jnp.where(x == 0, other, keep)], axis=1)


def input_taps(ny, depth, wt, buf, at):
    cells = buf.shape[1] - 2 * ny
    lanes = buf.shape[2] // 3
    acc = jnp.zeros((cells, wt.shape[1]), F32)
    for b in range(3):
        for c in range(3):
            lhs = buf[at, (2 - b) * ny : (2 - b) * ny + cells, c * lanes : (c + 1) * lanes]
            acc = acc + lax.dot_general(
                lhs, wt[depth * 9 + b * 3 + c], (((1,), (1,)), ((), ())), preferred_element_type=F32
            )
    return acc


def near_input_body(ny, pos, kn, on, kf, of, near, near_o, wt, act_n, act_f, out, partial, act, done, buf):
    odd, x = pos[0], pos[6]
    put_plane(buf, 0, whole(x, kn[...], on[...]), ny, True)
    put_plane(buf, 1, whole(x, kf[...], of[...]), ny, True)
    put_plane(buf, 2, whole(x, near[...], near_o[...]), ny, True)
    total = input_taps(ny, 1, wt, buf, 0) + input_taps(ny, 2 - 2 * odd, wt, buf, 1)
    out[...] = (total + input_taps(ny, 2 * odd, wt, buf, 2)).astype(BF)
    partial[...] = input_taps(ny, 1, wt, buf, 1) + input_taps(ny, 2 * odd, wt, buf, 0)
    done[...] = jnp.zeros_like(done)
    act[1 - odd] = act_n[...]
    act[odd] = act_f[...]


def far_input_body(inside, ny, pos, far, far_o, wt, partial, ig_n, out, done, buf):
    odd, x, mine = pos[0], pos[6], pos[2]
    beyond = whole(x, far[...], far_o[...])
    if inside:
        beyond = jnp.where((mine == 0) | (mine == 3), jnp.zeros_like(beyond), beyond)
    put_plane(buf, 0, beyond, ny, True)
    out[odd] = (partial[...] + input_taps(ny, 2 - 2 * odd, wt, buf, 0)).astype(BF)
    out[1 - odd] = ig_n[...]
    done[...] = jnp.zeros_like(done)


def per_device(volumes, weight, bias, cotangent):
    samples, planes, nx, ny, local_in = volumes.shape
    outputs = weight.shape[4]
    local_out = bias.shape[0]
    plane = nx * ny
    cells = planes * plane
    slabs = lax.axis_size("slab")
    s, z, y = lax.axis_index("slab"), lax.axis_index("dp"), lax.axis_index("chan")
    odd, mine, x = s % 2, s % 4, (s // 2) % 2
    beside = jnp.where((s == 0) | (s == slabs - 1), 0, 1)
    pos = jnp.stack([odd, y, mine, odd, z, z, x, beside]).astype(jnp.int32)
    factor = float(samples * cells * slabs * lax.axis_size("dp")) ** -0.5
    padded = plane + 2 * ny
    macs = plane * 27 * local_in * outputs

    def next_pair(value):
        pairs = [(i, i + 1) for i in range(1, slabs - 1, 2)]
        return lax.ppermute(value, "slab", pairs + [(j, i) for i, j in pairs])

    vol = volumes.reshape(planes, plane, local_in)
    w = weight.reshape(3, 9 * local_in, outputs)
    vol_n = jnp.where(odd == 0, vol[1], vol[0])
    vol_f = jnp.where(odd == 0, vol[0], vol[1])
    near, x_f = swap(vol_n, "slab", 1), swap(vol_f, "slab", 2)
    ends = group_ends(vol, slabs)
    wide, thin = ((plane, local_out), F32), ((plane, local_out), BF)
    one = [pltpu.VMEM((1, padded, 3 * local_in), BF)]
    own_n, send_n, kept, held, done_n = vmem_call(
        functools.partial(near_body, ny),
        [wide, thin, ((2, padded, 3 * local_in), BF), (w.shape, BF), ((8, 128), F32)],
        one + [pltpu.SemaphoreType.DMA(())],
        macs,
        pos, vol_n, vol_f, near, w,
    )
    recv_n = swap(send_n, "chan", 1)
    cx_f = swap(held_back(x_f, done_n), "slab", 1)
    beyond = cx_f
    if slabs > 4:
        beyond = jnp.where((mine == 0) | (mine == 3), next_pair(vol_f), beyond)
    own_f, send_f = vmem_call(functools.partial(far_body, ny), [wide, thin], one, macs, pos, beyond, kept, held)
    recv_f = swap(send_f, "chan", 1)

    bias_row, cot = bias.reshape(1, local_out), cotangent.reshape(planes, plane, local_out)
    act_n, g_n, vol_n2 = vmem_call(
        near_gate_body, [thin, thin, thin], [], 0, pos, own_n, recv_n, bias_row, cot, vol_n
    )
    x_n, core_vf = swap(vol_n2, "slab", 2), swap(vol_f, "slab", 1)
    cx_n = swap(x_n, "slab", 1)
    g_ny = swap(g_n, "chan", 1)
    vt = vmem_call(
        volume_body,
        [((4 * planes + 4, 3 * local_in // 2, plane), BF)],
        [],
        0,
        pos, vol_n, vol_f, near, core_vf, x_n, x_f, cx_n, cx_f, ends,
    )[0]
    act_f, g_f = vmem_call(far_gate_body, [thin, thin], [], 0, pos, own_f, recv_f, bias_row, cot, after=(g_n,))
    g_fy = swap(g_f, "chan", 1)
    lanes = 3 * local_out

    def routed(mine_g, other_g):
        keep, send = jnp.where(x == y, mine_g, other_g), jnp.where(x == y, other_g, mine_g)
        return keep, send, swap(send, "slab", 2)

    keep_n, send_n, got_n = routed(g_n, g_ny)
    core_n = swap(keep_n, "slab", 1), swap(got_n, "slab", 1)
    keep_f, send_f, got_f = routed(g_f, g_fy)
    acc_shape = (3, 3 * local_in // 2, lanes)
    core_f = swap(keep_f, "slab", 1)
    sums_of = [(acc_shape, F32), ((8, lanes), F32)]
    four, two = pltpu.VMEM((4, padded, lanes), BF), pltpu.VMEM((2, padded, lanes), BF)
    first = functools.partial(first_kernel_body, ny)
    acc0, total0 = vmem_call(first, sums_of, [four], 2 * macs, pos, vt, keep_n, core_n[0], keep_f, core_f)
    second = functools.partial(second_kernel_body, ny)
    acc0, total0 = vmem_call(second, sums_of, [two], macs, pos, vt, got_n, core_n[1], acc0, total0)
    last_f = swap(held_back(got_f, total0[:, :local_out]), "slab", 1)
    single = pltpu.VMEM((1, padded, lanes), BF)
    acc1, total1 = vmem_call(
        functools.partial(next_kernel_body, 2, ny), sums_of, [single], macs, pos, vt, got_f, acc0, total0
    )
    rows = 9 * local_in // 8
    cut = [((rows, lanes), F32), ((rows, lanes), BF), ((rows, lanes), F32), ((rows, lanes), BF)]
    if slabs == 4:
        keep, s1, s2, s3, total, sent = vmem_call(
            functools.partial(last_kernel_body, ny),
            cut + [((8, lanes), F32), thin],
            [single, pltpu.VMEM(acc_shape, F32)],
            macs,
            pos, vt, last_f, acc1, total1, keep_f,
        )
    else:
        acc, total = vmem_call(
            functools.partial(next_kernel_body, 3, ny), sums_of, [single], macs, pos, vt, last_f, acc1, total1
        )
        bit = 4
        while bit < slabs:
            acc, total = acc + swap(acc, "slab", bit), total + swap(total, "slab", bit)
            bit *= 2
        keep, s1, s2, s3 = vmem_call(cut_body, cut, [], 0, pos, acc)
        sent = keep_f
    r3, total_z = swap(s3, "dp", 1), swap(total, "dp", 1)
    merged, total_b = (s2 + r3.astype(F32)).astype(BF), total + total_z
    r2, r1, total_z2 = swap(merged, "dp", 2), swap(held_back(s1, total_z), "dp", 1), swap(total_b, "dp", 2)

    sent_x = swap(sent, "slab", 2)
    wt = weight.reshape(27, local_in, outputs)
    ig_buf = pltpu.VMEM((3, padded, 3 * outputs), BF)
    ig_n, partial, act, ig_n_done = vmem_call(
        functools.partial(near_input_body, ny),
        [
            ((plane, local_in), BF), ((plane, local_in), F32), ((planes, plane, local_out), BF), ((8, lanes), F32)
        ],
        [ig_buf],
        2 * macs,
        pos, keep_n, send_n, keep_f, send_f, core_n[0], swap(send_n, "slab", 1), wt, act_n, act_f,
        after=(merged, sent_x),
    )
    far_keep = last_f
    far_send = swap(sent_x, "slab", 1)
    if slabs > 4:
        edge = (mine == 0) | (mine == 3)
        far_keep = jnp.where(edge, next_pair(send_f), far_keep)
        far_send = jnp.where(edge, next_pair(keep_f), far_send)
    ig, ig_done = vmem_call(
        functools.partial(far_input_body, slabs == 4, ny),
        [((planes, plane, local_in), BF), ((8, lanes), F32)],
        [pltpu.VMEM((1, padded, 3 * outputs), BF)],
        0,
        pos, far_keep, far_send, wt, partial, ig_n,
    )
    quarter = held_back(((keep + r1.astype(F32) + r2.astype(F32)) * factor).astype(BF), ig_n_done)
    total3 = (total_b + total_z2) * factor
    q1, q2, x0 = swap(quarter, "dp", 1), swap(quarter, "dp", 2), swap(quarter, "slab", 2)
    total_x = swap(total3, "slab", 2)
    out_shape = (27, local_in, outputs)
    token = (8, lanes), F32
    one_z, two_x, four_c = vmem_call(
        round_body,
        [(quarter.shape, BF), ((2,) + quarter.shape, BF), ((4,) + quarter.shape, BF)],
        [],
        0,
        pos, quarter, q1, x0, q2,
        after=(total_x,),
    )
    q3, x12, core = swap(one_z, "dp", 1), swap(two_x, "slab", 2), swap(four_c, "slab", 1)
    out, done = spread(first_spread_body, out_shape, token, (), pos, four_c, core)
    one_x, three_c = vmem_call(
        next_round_body, [(quarter.shape, BF), ((3,) + quarter.shape, BF)], [], 0, pos, q3, x12, after=(done, ig_done)
    )
    x3, core_b = swap(one_x, "slab", 2), swap(three_c, "slab", 1)
    out, done = spread(next_spread_body, out_shape, token, (), pos, three_c, core_b, out, alias=True)
    core_x3 = swap(held_back(x3, done), "slab", 1)
    weight_grad, _ = spread(last_spread_body, out_shape, token, (), pos, x3, core_x3, out, alias=True)
    bias_grad = jnp.where(x == y, total3, total_x)[0, :local_out]
    shape = (samples, planes, nx, ny)
    return (
        act.reshape(shape + (local_out,)),
        ig.reshape(shape + (local_in,)),
        weight_grad.reshape(weight.shape),
        bias_grad,
    )


def group_ends(vol, slabs):
    before, after = jnp.zeros_like(vol[0]), jnp.zeros_like(vol[0])
    for group in range(4 if slabs > 4 else 0):
        up = [(i - 1, i + group) for i in range(4, slabs, 4)]
        down = [(i + 4, i + group) for i in range(0, slabs - 4, 4)]
        before = before + lax.ppermute(vol[vol.shape[0] - 1], "slab", up)
        after = after + lax.ppermute(vol[0], "slab", down)
    return jnp.stack([before, after])


def solution(mesh):
    placed = (
        P("dp", "slab", None, None, "chan"),
        P(None, None, None, "chan", None),
        P("chan"),
        P("dp", "slab", None, None, "chan"),
    )
    return jax.shard_map(
        per_device,
        mesh=mesh,
        in_specs=placed,
        out_specs=(
            P("dp", "slab", None, None, "chan"),
            P("dp", "slab", None, None, "chan"),
            P(None, None, None, "chan", None),
            P("chan"),
        ),
        check_vma=False,
    )
```

```python
import functools

import jax
import jax.numpy as jnp
from jax import lax
from jax.experimental import pallas as pl
from jax.experimental.pallas import tpu as pltpu
from jax.sharding import PartitionSpec as P

BF = jnp.bfloat16
F32 = jnp.float32
MIB = 1 << 20


def swap(value, axis, bit):
    return lax.ppermute(value, axis, [(i, i ^ bit) for i in range(lax.axis_size(axis))])


def vmem_call(body, outs, scratch, flops, *args, left=(), after=(), limit=20):
    shapes = [jax.ShapeDtypeStruct(s, d) for s, d in outs]
    count, waited = len(args), len(after)

    def inner(*refs):
        body(*refs[:count], *refs[count + waited :])

    specs = [pl.BlockSpec(memory_space=pl.ANY if n in left else pltpu.VMEM) for n in range(1, count)]
    return pl.pallas_call(
        inner,
        out_shape=shapes,
        in_specs=[pl.BlockSpec(memory_space=pltpu.SMEM)] + specs + [pl.BlockSpec(memory_space=pl.ANY)] * waited,
        out_specs=[pl.BlockSpec(memory_space=pltpu.VMEM)] * len(shapes),
        scratch_shapes=scratch,
        compiler_params=pltpu.CompilerParams(vmem_limit_bytes=limit * MIB),
        cost_estimate=pl.CostEstimate(flops=4 * flops + 10**9, bytes_accessed=MIB, transcendentals=0),
    )(*args, *after)


def shift_y(value, step, ny):
    rows = value.shape[0]
    y = lax.broadcasted_iota(jnp.int32, value.shape, 0) % ny
    rolled = pltpu.roll(value, (-step) % rows, 0)
    return jnp.where(y == (0 if step < 0 else ny - 1), 0.0, rolled)


def put_plane(buf, at, value, ny, flip):
    cells, lanes = value.shape
    wide = value.astype(F32)
    edge = jnp.zeros((ny, 3 * lanes), BF)
    buf[at, 0:ny, :] = edge
    buf[at, ny + cells : 2 * ny + cells, :] = edge
    for c in range(3):
        step = (1 - c) if flip else (c - 1)
        moved = value if step == 0 else shift_y(wide, step, ny).astype(BF)
        buf[at, ny : ny + cells, c * lanes : (c + 1) * lanes] = moved


def near_body(ny, pos, vol_n, vol_f, plane, w, own, send, kept, held, done, buf, sem):
    copy = pltpu.make_async_copy(w, held, sem)
    copy.start()
    put_plane(kept, 0, vol_n[...], ny, False)
    put_plane(kept, 1, vol_f[...], ny, False)
    put_plane(buf, 0, plane[...], ny, False)
    sums(ny, pos, kept.at[0], kept.at[1], buf.at[0], 2 - 2 * pos[0], w, own, send)
    done[...] = jnp.zeros_like(done)
    copy.wait()


def far_body(ny, pos, beyond, kept, w, own, send, buf):
    odd = pos[0]
    put_plane(buf, 0, jnp.where(pos[7] == 0, 0.0, beyond[...].astype(F32)).astype(BF), ny, False)
    sums(ny, pos, kept.at[1], kept.at[0], buf.at[0], 2 * odd, w, own, send)


def sums(ny, pos, middle, inner, outer, depth, w, own, send):
    cells = own.shape[0]
    y, half = pos[1], own.shape[1]
    total = tap(middle, w, 1, ny, cells) + tap(inner, w, 2 - depth, ny, cells) + tap(outer, w, depth, ny, cells)
    own[...] = jnp.where(y == 0, total[:, :half], total[:, half:])
    send[...] = jnp.where(y == 0, total[:, half:], total[:, :half]).astype(BF)


def tap(field, w, depth, ny, cells):
    lhs = jnp.concatenate([field[b * ny : b * ny + cells, :] for b in range(3)], axis=1)
    return jnp.dot(lhs, w[depth], preferred_element_type=F32)


def gate(pos, plane, own, recv, bias, cot):
    pre = own[...] + recv[...].astype(F32) + bias[...].astype(F32)
    s = 1.0 / (1.0 + jnp.exp(-pre))
    return (pre * s).astype(BF), (cot[plane].astype(F32) * s * (1.0 + pre * (1.0 - s))).astype(BF)


def near_gate_body(pos, own, recv, bias, cot, vol_n, act, grad, vol_out):
    act[...], grad[...] = gate(pos, 1 - pos[0], own, recv, bias, cot)
    vol_out[...] = vol_n[...]


def far_gate_body(pos, own, recv, bias, cot, act, grad):
    act[...], grad[...] = gate(pos, pos[0], own, recv, bias, cot)


def held_back(value, *tokens):
    rows, lanes = value.shape
    ready = functools.reduce(jnp.logical_and, [token == token for token in tokens])
    blocks = value.reshape(rows // 8, 8, lanes)
    return jnp.where(ready[None], blocks, jnp.zeros_like(blocks)).reshape(rows, lanes)


def volume_body(pos, n0, f0, n1, f1, n2, f2, n3, f3, ends, vt):
    lanes = n0.shape[1]
    mine, k, odd = pos[2], pos[3], pos[0]
    keep = lanes // 2

    def put(at, value):
        turned = value.astype(F32).T
        turned = jnp.where(k == 0, turned[:keep], turned[keep:]).astype(BF)
        for a in range(3):
            vt[at + 2 - a, a * keep : (a + 1) * keep, :] = turned

    put(0, ends[0])
    put(9, ends[1])
    for who, (near, far) in enumerate(((n0, f0), (n1, f1), (n2, f2), (n3, f3))):
        own_odd = odd if who in (0, 2) else 1 - odd
        put((mine ^ who) * 2 + (1 - own_odd) + 1, near[...])
        put((mine ^ who) * 2 + own_odd + 1, far[...])


def kernel_terms(ny, pos, vt, grads, buf, acc, before):
    cells, lanes = grads[0][2].shape
    mine, odd = pos[2], pos[0]
    bsum = jnp.zeros((1, lanes), F32)
    where = []
    for n, (far, who, ref) in enumerate(grads):
        own_odd = odd if who in (0, 2) else 1 - odd
        where.append((mine ^ who) * 2 + (own_odd if far else 1 - own_odd) + 2)
        value = ref[...]
        put_plane(buf, n, value, ny, True)
        bsum = bsum + jnp.sum(value.astype(F32), axis=0, keepdims=True)
    lhs = jnp.concatenate([vt[at] for at in where], axis=1)
    for b in range(3):
        rhs = [buf[n, (2 - b) * ny : (2 - b) * ny + cells, :] for n in range(len(grads))]
        summed = jnp.dot(lhs, jnp.concatenate(rhs, axis=0), preferred_element_type=F32)
        acc[b] = summed if before is None else summed + before[b]
    return bsum


def first_kernel_body(ny, pos, vt, g0, g1, f0, f1, acc, total, buf):
    grads = ((0, 0, g0), (0, 1, g1), (1, 0, f0), (1, 1, f1))
    bsum = kernel_terms(ny, pos, vt, grads, buf, acc, None)
    total[...] = jnp.broadcast_to(jnp.concatenate([bsum] * 3, axis=1), total.shape)


def second_kernel_body(ny, pos, vt, g2, g3, acc0, total0, acc, total, buf):
    bsum = kernel_terms(ny, pos, vt, ((0, 2, g2), (0, 3, g3)), buf, acc, acc0)
    total[...] = total0[...] + jnp.concatenate([bsum] * 3, axis=1)


def next_kernel_body(who, ny, pos, vt, f, acc0, total0, acc, total, buf):
    bsum = kernel_terms(ny, pos, vt, ((1, who, f),), buf, acc, acc0)
    total[...] = total0[...] + jnp.concatenate([bsum] * 3, axis=1)


def last_kernel_body(ny, pos, vt, f3, acc0, total0, kf, keep, s1, s2, s3, total, sent, buf, acc):
    sent[...] = kf[...]
    next_kernel_body(3, ny, pos, vt, f3, acc0, total0, acc, total, buf)
    cut_body(pos, acc, keep, s1, s2, s3)


def cut_body(pos, acc, keep, s1, s2, s3):
    part = keep.shape[0] // 9
    mine = pos[4]
    for b in range(3):
        for a in range(3):
            rows = slice((3 * b + a) * part, (3 * b + a + 1) * part)
            for who, ref in ((0, keep), (1, s1), (2, s2), (3, s3)):
                at = pl.multiple_of((4 * a + (mine ^ who)) * part, part)
                ref[rows, :] = acc[b, pl.ds(at, part), :].astype(ref.dtype)


def split_rows(total):
    value = jnp.broadcast_to(total[0:1, :], (16, total.shape[1]))
    high = value.astype(BF)
    rest = value - high.astype(F32)
    mid = rest.astype(BF)
    low = (rest - mid.astype(F32)).astype(BF)
    return jnp.concatenate([high, mid, low], axis=1)


def place(pos, pieces, out, wide, sems):
    x, k, mine = pos[6], pos[3], pos[4]
    half = out.shape[2] // 2
    copies = []
    for n, (who, j, piece) in enumerate(pieces):
        for b in range(3):
            for a in range(3):
                for c in range(3):
                    rows = slice((3 * b + a) * 16, (3 * b + a + 1) * 16)
                    wide[n, (a * 3 + b) * 3 + c] = piece[rows, c * half : (c + 1) * half].astype(F32)
        row = pl.multiple_of((k ^ (who >> 1)) * 64 + (mine ^ j) * 16, 16)
        lane = pl.multiple_of((x ^ (who & 1)) * half, half)
        copy = pltpu.make_async_copy(wide.at[n], out.at[:, pl.ds(row, 16), pl.ds(lane, half)], sems.at[n])
        copy.start()
        copies.append(copy)
    for copy in copies:
        copy.wait()


def round_body(pos, q, x0, q1, q2, one_z, one_x, x0_z, four_c):
    one_z[...], one_x[...], x0_z[...] = q2[...], q2[...], x0[...]
    four_c[0], four_c[1], four_c[2], four_c[3] = q[...], q1[...], q2[...], x0[...]


def next_round_body(pos, q3, x2, total, last_x, two_c):
    rows = q3.shape[0]
    last_x[0:rows, :] = q3[...]
    last_x[rows : rows + 16, :] = split_rows(total[:, : total.shape[1] // 3])
    two_c[0], two_c[1] = q3[...], x2[...]


def both_cores(kinds, own, core):
    pieces = [(who, j, own.at[n]) for n, (who, j) in enumerate(kinds)]
    return pieces + [(who + 2, j, core.at[n]) for n, (who, j) in enumerate(kinds)]


def first_spread_body(pos, own, core, out, done, wide, sems):
    place(pos, both_cores(((0, 0), (0, 1), (0, 2), (1, 0)), own, core), out, wide, sems)
    done[...] = jnp.zeros_like(done)


def next_spread_body(pos, own, core, before, out, done, wide, sems):
    place(pos, both_cores(((0, 3), (1, 2)), own, core), out, wide, sems)
    done[...] = jnp.zeros_like(done)


def last_spread_body(pos, own, core, before, out, done, wide, sems):
    rows = own.shape[0] // 2
    pieces = []
    for n, (who, j) in enumerate(((1, 1), (1, 3))):
        pieces.append((who, j, own.at[n * rows : (n + 1) * rows]))
        pieces.append((who + 2, j, core.at[n * rows : (n + 1) * rows]))
    place(pos, pieces, out, wide, sems)
    done[...] = jnp.zeros_like(done)


def spread(body, shape, small, after, pos, *arrays, alias=False):
    whole = pl.BlockSpec(memory_space=pltpu.VMEM)
    anywhere = pl.BlockSpec(memory_space=pl.ANY)
    count, waited = 1 + len(arrays), len(after)

    def inner(*refs):
        body(*refs[:count], *refs[count + waited :])

    specs = [pl.BlockSpec(memory_space=pltpu.SMEM)] + [whole] * (len(arrays) - alias) + [anywhere] * alias
    return pl.pallas_call(
        inner,
        out_shape=[jax.ShapeDtypeStruct(shape, F32), jax.ShapeDtypeStruct(*small)],
        in_specs=specs + [anywhere] * waited,
        out_specs=[anywhere, whole],
        scratch_shapes=[pltpu.VMEM((8, shape[0], 16, shape[2] // 2), F32), pltpu.SemaphoreType.DMA((8,))],
        input_output_aliases={count - 1: 0} if alias else {},
        compiler_params=pltpu.CompilerParams(vmem_limit_bytes=20 * MIB),
        cost_estimate=pl.CostEstimate(flops=1, bytes_accessed=1, transcendentals=0),
    )(pos, *arrays, *after)


def whole(x, keep, other):
    first = jnp.where(x == 0, keep, other)
    return jnp.concatenate([first, jnp.where(x == 0, other, keep)], axis=1)


def input_taps(ny, depths, wt, buf, at):
    cells = buf.shape[1] - 2 * ny
    lanes = buf.shape[2] // 3
    acc = jnp.zeros((cells, len(depths) * wt.shape[1]), F32)
    for b in range(3):
        for c in range(3):
            lhs = buf[at, (2 - b) * ny : (2 - b) * ny + cells, c * lanes : (c + 1) * lanes]
            rhs = jnp.concatenate([wt[depth * 9 + b * 3 + c] for depth in depths], axis=0)
            acc = acc + lax.dot_general(lhs, rhs, (((1,), (1,)), ((), ())), preferred_element_type=F32)
    return acc


def near_input_body(ny, pos, kn, on, kf, of, near, near_o, wt, act_n, act_f, out, partial, act, done, buf):
    odd, x = pos[0], pos[6]
    put_plane(buf, 0, whole(x, kn[...], on[...]), ny, True)
    put_plane(buf, 1, whole(x, kf[...], of[...]), ny, True)
    put_plane(buf, 2, whole(x, near[...], near_o[...]), ny, True)
    half = out.shape[1]
    both = input_taps(ny, (1, 2 * odd), wt, buf, 0)
    swapped = input_taps(ny, (2 - 2 * odd, 1), wt, buf, 1)
    out[...] = (both[:, :half] + swapped[:, :half] + input_taps(ny, (2 * odd,), wt, buf, 2)).astype(BF)
    partial[...] = both[:, half:] + swapped[:, half:]
    done[...] = jnp.zeros_like(done)
    act[1 - odd] = act_n[...]
    act[odd] = act_f[...]


def far_input_body(inside, ny, pos, far, far_o, wt, partial, ig_n, out, done, buf):
    odd, x, mine = pos[0], pos[6], pos[2]
    beyond = whole(x, far[...], far_o[...])
    if inside:
        beyond = jnp.where((mine == 0) | (mine == 3), jnp.zeros_like(beyond), beyond)
    put_plane(buf, 0, beyond, ny, True)
    out[odd] = (partial[...] + input_taps(ny, (2 - 2 * odd,), wt, buf, 0)).astype(BF)
    out[1 - odd] = ig_n[...]
    done[...] = jnp.zeros_like(done)


def per_device(volumes, weight, bias, cotangent):
    samples, planes, nx, ny, local_in = volumes.shape
    outputs = weight.shape[4]
    local_out = bias.shape[0]
    plane = nx * ny
    cells = planes * plane
    slabs = lax.axis_size("slab")
    s, z, y = lax.axis_index("slab"), lax.axis_index("dp"), lax.axis_index("chan")
    odd, mine, x = s % 2, s % 4, (s // 2) % 2
    beside = jnp.where((s == 0) | (s == slabs - 1), 0, 1)
    pos = jnp.stack([odd, y, mine, odd, z, z, x, beside]).astype(jnp.int32)
    factor = float(samples * cells * slabs * lax.axis_size("dp")) ** -0.5
    padded = plane + 2 * ny
    macs = plane * 27 * local_in * outputs

    def next_pair(value):
        pairs = [(i, i + 1) for i in range(1, slabs - 1, 2)]
        return lax.ppermute(value, "slab", pairs + [(j, i) for i, j in pairs])

    vol = volumes.reshape(planes, plane, local_in)
    w = weight.reshape(3, 9 * local_in, outputs)
    vol_n = jnp.where(odd == 0, vol[1], vol[0])
    vol_f = jnp.where(odd == 0, vol[0], vol[1])
    near, x_f = swap(vol_n, "slab", 1), swap(vol_f, "slab", 2)
    ends = group_ends(vol, slabs)
    wide, thin = ((plane, local_out), F32), ((plane, local_out), BF)
    one = [pltpu.VMEM((1, padded, 3 * local_in), BF)]
    own_n, send_n, kept, held, done_n = vmem_call(
        functools.partial(near_body, ny),
        [wide, thin, ((2, padded, 3 * local_in), BF), (w.shape, BF), ((8, 128), F32)],
        one + [pltpu.SemaphoreType.DMA(())],
        macs,
        pos, vol_n, vol_f, near, w,
    )
    recv_n = swap(send_n, "chan", 1)
    cx_f = swap(held_back(x_f, done_n), "slab", 1)
    beyond = cx_f
    if slabs > 4:
        beyond = jnp.where((mine == 0) | (mine == 3), next_pair(vol_f), beyond)
    own_f, send_f = vmem_call(functools.partial(far_body, ny), [wide, thin], one, macs, pos, beyond, kept, held)
    recv_f = swap(send_f, "chan", 1)

    bias_row, cot = bias.reshape(1, local_out), cotangent.reshape(planes, plane, local_out)
    act_n, g_n, vol_n2 = vmem_call(
        near_gate_body, [thin, thin, thin], [], 0, pos, own_n, recv_n, bias_row, cot, vol_n
    )
    x_n, core_vf = swap(vol_n2, "slab", 2), swap(vol_f, "slab", 1)
    cx_n = swap(x_n, "slab", 1)
    g_ny = swap(g_n, "chan", 1)
    vt = vmem_call(
        volume_body,
        [((4 * planes + 4, 3 * local_in // 2, plane), BF)],
        [],
        0,
        pos, vol_n, vol_f, near, core_vf, x_n, x_f, cx_n, cx_f, ends,
    )[0]
    act_f, g_f = vmem_call(far_gate_body, [thin, thin], [], 0, pos, own_f, recv_f, bias_row, cot, after=(g_n,))
    g_fy = swap(g_f, "chan", 1)
    lanes = 3 * local_out

    def routed(mine_g, other_g):
        keep, send = jnp.where(x == y, mine_g, other_g), jnp.where(x == y, other_g, mine_g)
        return keep, send, swap(send, "slab", 2)

    keep_n, send_n, got_n = routed(g_n, g_ny)
    core_n = swap(keep_n, "slab", 1), swap(got_n, "slab", 1)
    keep_f, send_f, got_f = routed(g_f, g_fy)
    acc_shape = (3, 3 * local_in // 2, lanes)
    core_f = swap(keep_f, "slab", 1)
    sums_of = [(acc_shape, F32), ((8, lanes), F32)]
    four, two = pltpu.VMEM((4, padded, lanes), BF), pltpu.VMEM((2, padded, lanes), BF)
    first = functools.partial(first_kernel_body, ny)
    acc0, total0 = vmem_call(first, sums_of, [four], 2 * macs, pos, vt, keep_n, core_n[0], keep_f, core_f)
    second = functools.partial(second_kernel_body, ny)
    acc0, total0 = vmem_call(second, sums_of, [two], macs, pos, vt, got_n, core_n[1], acc0, total0)
    last_f = swap(held_back(got_f, total0[:, :local_out]), "slab", 1)
    single = pltpu.VMEM((1, padded, lanes), BF)
    acc1, total1 = vmem_call(
        functools.partial(next_kernel_body, 2, ny), sums_of, [single], macs, pos, vt, got_f, acc0, total0
    )
    rows = 9 * local_in // 8
    cut = [((rows, lanes), F32), ((rows, lanes), BF), ((rows, lanes), F32), ((rows, lanes), BF)]
    if slabs == 4:
        keep, s1, s2, s3, total, sent = vmem_call(
            functools.partial(last_kernel_body, ny),
            cut + [((8, lanes), F32), thin],
            [single, pltpu.VMEM(acc_shape, F32)],
            macs,
            pos, vt, last_f, acc1, total1, keep_f,
        )
    else:
        acc, total = vmem_call(
            functools.partial(next_kernel_body, 3, ny), sums_of, [single], macs, pos, vt, last_f, acc1, total1
        )
        bit = 4
        while bit < slabs:
            acc, total = acc + swap(acc, "slab", bit), total + swap(total, "slab", bit)
            bit *= 2
        keep, s1, s2, s3 = vmem_call(cut_body, cut, [], 0, pos, acc)
        sent = keep_f
    r3, r1, total_z2 = swap(s3, "dp", 1), swap(s1, "dp", 1), swap(total, "dp", 2)
    merged, total_a = (s2 + r3.astype(F32)).astype(BF), total + total_z2
    r2 = swap(merged, "dp", 2)

    sent_x = swap(sent, "slab", 2)
    wt = weight.reshape(27, local_in, outputs)
    ig_buf = pltpu.VMEM((3, padded, 3 * outputs), BF)
    ig_n, partial, act, ig_n_done = vmem_call(
        functools.partial(near_input_body, ny),
        [
            ((plane, local_in), BF), ((plane, local_in), F32), ((planes, plane, local_out), BF), ((8, lanes), F32)
        ],
        [ig_buf],
        2 * macs,
        pos, keep_n, send_n, keep_f, send_f, core_n[0], swap(send_n, "slab", 1), wt, act_n, act_f,
        after=(merged, sent_x),
    )
    far_keep = last_f
    far_send = swap(sent_x, "slab", 1)
    if slabs > 4:
        edge = (mine == 0) | (mine == 3)
        far_keep = jnp.where(edge, next_pair(send_f), far_keep)
        far_send = jnp.where(edge, next_pair(keep_f), far_send)
    ig, ig_done = vmem_call(
        functools.partial(far_input_body, slabs == 4, ny),
        [((planes, plane, local_in), BF), ((8, lanes), F32)],
        [pltpu.VMEM((1, padded, 3 * outputs), BF)],
        0,
        pos, far_keep, far_send, wt, partial, ig_n,
    )
    quarter = held_back(((keep + r1.astype(F32) + r2.astype(F32)) * factor).astype(BF), ig_n_done, total_z2)
    total_z1 = swap(total_a, "dp", 1)
    q1, q2, x0 = swap(quarter, "dp", 1), swap(quarter, "dp", 2), swap(quarter, "slab", 2)
    total_b = total_a + total_z1
    out_shape = (27, local_in, outputs)
    token = (8, lanes), F32
    one_z, one_x, x0_z, four_c = vmem_call(
        round_body,
        [(quarter.shape, BF)] * 3 + [((4,) + quarter.shape, BF)],
        [],
        0,
        pos, quarter, x0, q1, q2,
        after=(total_z1, ig_done),
    )
    q3, x2, x1, core = swap(one_z, "dp", 1), swap(one_x, "slab", 2), swap(x0_z, "dp", 1), swap(four_c, "slab", 1)
    out, done = spread(first_spread_body, out_shape, token, (), pos, four_c, core)
    last_x, two_c = vmem_call(
        next_round_body,
        [((rows + 16, lanes), BF), ((2,) + quarter.shape, BF)],
        [],
        0,
        pos, q3, x2, total_b,
        after=(done,),
    )
    x3, core_b = swap(last_x, "slab", 2), swap(two_c, "slab", 1)
    out, done = spread(next_spread_body, out_shape, token, (), pos, two_c, core_b, out, alias=True)
    x3 = held_back(x3, done)
    pair_x = jnp.concatenate([x1, x3[:rows]], axis=0)
    core_x = swap(pair_x, "slab", 1)
    weight_grad, _ = spread(last_spread_body, out_shape, token, (), pos, pair_x, core_x, out, alias=True)
    tail = x3[rows : rows + 1].astype(F32).reshape(3, local_out)
    bias_grad = jnp.where(x == y, total_b[0, :local_out], tail[0] + tail[1] + tail[2]) * factor
    shape = (samples, planes, nx, ny)
    return (
        act.reshape(shape + (local_out,)),
        ig.reshape(shape + (local_in,)),
        weight_grad.reshape(weight.shape),
        bias_grad,
    )


def group_ends(vol, slabs):
    before, after = jnp.zeros_like(vol[0]), jnp.zeros_like(vol[0])
    for group in range(4 if slabs > 4 else 0):
        up = [(i - 1, i + group) for i in range(4, slabs, 4)]
        down = [(i + 4, i + group) for i in range(0, slabs - 4, 4)]
        before = before + lax.ppermute(vol[vol.shape[0] - 1], "slab", up)
        after = after + lax.ppermute(vol[0], "slab", down)
    return jnp.stack([before, after])


def solution(mesh):
    placed = (
        P("dp", "slab", None, None, "chan"),
        P(None, None, None, "chan", None),
        P("chan"),
        P("dp", "slab", None, None, "chan"),
    )
    return jax.shard_map(
        per_device,
        mesh=mesh,
        in_specs=placed,
        out_specs=(
            P("dp", "slab", None, None, "chan"),
            P("dp", "slab", None, None, "chan"),
            P(None, None, None, "chan", None),
            P("chan"),
        ),
        check_vma=False,
    )
```

```python
import functools

import jax
import jax.numpy as jnp
from jax import lax
from jax.experimental import pallas as pl
from jax.experimental.pallas import tpu as pltpu
from jax.sharding import PartitionSpec as P

BF = jnp.bfloat16
F32 = jnp.float32
MIB = 1 << 20


def swap(value, axis, bit):
    return lax.ppermute(value, axis, [(i, i ^ bit) for i in range(lax.axis_size(axis))])


def position():
    s, z, y = lax.axis_index("slab"), lax.axis_index("dp"), lax.axis_index("chan")
    odd = s & 1
    beside = jnp.where((s == 0) | (s == lax.axis_size("slab") - 1), 0, 1)
    return odd, y, s & 3, odd, z, z, (s >> 1) & 1, beside


def vmem_call(body, outs, scratch, flops, *args, after=(), limit=20):
    shapes = [jax.ShapeDtypeStruct(s, d) for s, d in outs]
    count, waited = len(args), len(after)

    def inner(*refs):
        body(position(), *refs[:count], *refs[count + waited :])

    return pl.pallas_call(
        inner,
        out_shape=shapes,
        in_specs=[pl.BlockSpec(memory_space=pltpu.VMEM)] * count + [pl.BlockSpec(memory_space=pl.ANY)] * waited,
        out_specs=[pl.BlockSpec(memory_space=pltpu.VMEM)] * len(shapes),
        scratch_shapes=scratch,
        compiler_params=pltpu.CompilerParams(vmem_limit_bytes=limit * MIB),
        cost_estimate=pl.CostEstimate(flops=4 * flops + 10**9, bytes_accessed=MIB, transcendentals=0),
    )(*args, *after)


def shift_y(value, step, ny):
    rows = value.shape[0]
    y = lax.broadcasted_iota(jnp.int32, value.shape, 0) % ny
    rolled = pltpu.roll(value, (-step) % rows, 0)
    return jnp.where(y == (0 if step < 0 else ny - 1), 0.0, rolled)


def put_plane(buf, at, value, ny, flip):
    cells, lanes = value.shape
    wide = value.astype(F32)
    edge = jnp.zeros((ny, 3 * lanes), BF)
    buf[at, 0:ny, :] = edge
    buf[at, ny + cells : 2 * ny + cells, :] = edge
    for c in range(3):
        step = (1 - c) if flip else (c - 1)
        moved = value if step == 0 else shift_y(wide, step, ny).astype(BF)
        buf[at, ny : ny + cells, c * lanes : (c + 1) * lanes] = moved


def near_body(ny, pos, vol_n, vol_f, plane, w, own, send, kept, held, done, buf, sem):
    copy = pltpu.make_async_copy(w, held, sem)
    copy.start()
    put_plane(kept, 0, vol_n[...], ny, False)
    put_plane(kept, 1, vol_f[...], ny, False)
    put_plane(buf, 0, plane[...], ny, False)
    sums(ny, pos, kept.at[0], kept.at[1], buf.at[0], 2 - 2 * pos[0], w, own, send)
    done[...] = jnp.zeros_like(done)
    copy.wait()


def far_body(ny, pos, beyond, kept, w, own, send, buf):
    odd = pos[0]
    put_plane(buf, 0, jnp.where(pos[7] == 0, 0.0, beyond[...].astype(F32)).astype(BF), ny, False)
    sums(ny, pos, kept.at[1], kept.at[0], buf.at[0], 2 * odd, w, own, send)


def sums(ny, pos, middle, inner, outer, depth, w, own, send):
    cells = own.shape[0]
    y, half = pos[1], own.shape[1]
    total = tap(middle, w, 1, ny, cells) + tap(inner, w, 2 - depth, ny, cells) + tap(outer, w, depth, ny, cells)
    own[...] = jnp.where(y == 0, total[:, :half], total[:, half:])
    send[...] = jnp.where(y == 0, total[:, half:], total[:, :half]).astype(BF)


def tap(field, w, depth, ny, cells):
    lhs = jnp.concatenate([field[b * ny : b * ny + cells, :] for b in range(3)], axis=1)
    return jnp.dot(lhs, w[depth], preferred_element_type=F32)


def gate(pos, plane, own, recv, bias, cot):
    pre = own[...] + recv[...].astype(F32) + bias[...].astype(F32)
    s = 1.0 / (1.0 + jnp.exp(-pre))
    return (pre * s).astype(BF), (cot[plane].astype(F32) * s * (1.0 + pre * (1.0 - s))).astype(BF)


def near_gate_body(pos, own, recv, bias, cot, vol_n, act, grad, vol_out):
    act[...], grad[...] = gate(pos, 1 - pos[0], own, recv, bias, cot)
    vol_out[...] = vol_n[...]


def far_gate_body(pos, own, recv, bias, cot, act, grad):
    act[...], grad[...] = gate(pos, pos[0], own, recv, bias, cot)


def held_back(value, *tokens):
    rows, lanes = value.shape
    ready = functools.reduce(jnp.logical_and, [token == token for token in tokens])
    blocks = value.reshape(rows // 8, 8, lanes)
    return jnp.where(ready[None], blocks, jnp.zeros_like(blocks)).reshape(rows, lanes)


def volume_body(pos, n0, f0, n1, f1, n2, f2, n3, f3, ends, vt):
    lanes = n0.shape[1]
    mine, k, odd = pos[2], pos[3], pos[0]
    keep = lanes // 2

    def put(at, value):
        turned = value.astype(F32).T
        turned = jnp.where(k == 0, turned[:keep], turned[keep:]).astype(BF)
        for a in range(3):
            vt[at + 2 - a, a * keep : (a + 1) * keep, :] = turned

    put(0, ends[0])
    put(9, ends[1])
    for who, (near, far) in enumerate(((n0, f0), (n1, f1), (n2, f2), (n3, f3))):
        own_odd = odd if who in (0, 2) else 1 - odd
        put((mine ^ who) * 2 + (1 - own_odd) + 1, near[...])
        put((mine ^ who) * 2 + own_odd + 1, far[...])


def kernel_terms(ny, pos, vt, grads, buf, acc, before):
    cells, lanes = grads[0][2].shape
    mine, odd = pos[2], pos[0]
    bsum = jnp.zeros((1, lanes), F32)
    where = []
    for n, (far, who, ref) in enumerate(grads):
        own_odd = odd if who in (0, 2) else 1 - odd
        where.append((mine ^ who) * 2 + (own_odd if far else 1 - own_odd) + 2)
        value = ref[...]
        put_plane(buf, n, value, ny, True)
        bsum = bsum + jnp.sum(value.astype(F32), axis=0, keepdims=True)
    lhs = jnp.concatenate([vt[at] for at in where], axis=1)
    for b in range(3):
        rhs = [buf[n, (2 - b) * ny : (2 - b) * ny + cells, :] for n in range(len(grads))]
        summed = jnp.dot(lhs, jnp.concatenate(rhs, axis=0), preferred_element_type=F32)
        acc[b] = summed if before is None else summed + before[b]
    return bsum


def first_kernel_body(ny, pos, vt, g0, g1, f0, f1, acc, total, buf):
    grads = ((0, 0, g0), (0, 1, g1), (1, 0, f0), (1, 1, f1))
    bsum = kernel_terms(ny, pos, vt, grads, buf, acc, None)
    total[...] = jnp.broadcast_to(jnp.concatenate([bsum] * 3, axis=1), total.shape)


def second_kernel_body(ny, pos, vt, g2, g3, acc0, total0, acc, total, buf):
    bsum = kernel_terms(ny, pos, vt, ((0, 2, g2), (0, 3, g3)), buf, acc, acc0)
    total[...] = total0[...] + jnp.concatenate([bsum] * 3, axis=1)


def next_kernel_body(who, ny, pos, vt, f, acc0, total0, acc, total, buf):
    bsum = kernel_terms(ny, pos, vt, ((1, who, f),), buf, acc, acc0)
    total[...] = total0[...] + jnp.concatenate([bsum] * 3, axis=1)


def last_kernel_body(ny, pos, vt, f3, acc0, total0, kf, keep, s1, s2, s3, total, sent, buf, acc):
    sent[...] = kf[...]
    next_kernel_body(3, ny, pos, vt, f3, acc0, total0, acc, total, buf)
    cut_body(pos, acc, keep, s1, s2, s3)


def cut_body(pos, acc, keep, s1, s2, s3):
    part = keep.shape[0] // 9
    mine = pos[4]
    for b in range(3):
        for a in range(3):
            rows = slice((3 * b + a) * part, (3 * b + a + 1) * part)
            for who, ref in ((0, keep), (1, s1), (2, s2), (3, s3)):
                at = pl.multiple_of((4 * a + (mine ^ who)) * part, part)
                ref[rows, :] = acc[b, pl.ds(at, part), :].astype(ref.dtype)


def split_rows(total):
    value = jnp.broadcast_to(total[0:1, :], (16, total.shape[1]))
    high = value.astype(BF)
    rest = value - high.astype(F32)
    mid = rest.astype(BF)
    low = (rest - mid.astype(F32)).astype(BF)
    return jnp.concatenate([high, mid, low], axis=1)


def place(pos, pieces, out, wide, sems):
    x, k, mine = pos[6], pos[3], pos[4]
    half = out.shape[2] // 2
    copies = []
    for n, (who, j, piece) in enumerate(pieces):
        for b in range(3):
            for a in range(3):
                for c in range(3):
                    rows = slice((3 * b + a) * 16, (3 * b + a + 1) * 16)
                    wide[n, (a * 3 + b) * 3 + c] = piece[rows, c * half : (c + 1) * half].astype(F32)
        row = pl.multiple_of((k ^ (who >> 1)) * 64 + (mine ^ j) * 16, 16)
        lane = pl.multiple_of((x ^ (who & 1)) * half, half)
        copy = pltpu.make_async_copy(wide.at[n], out.at[:, pl.ds(row, 16), pl.ds(lane, half)], sems.at[n])
        copy.start()
        copies.append(copy)
    for copy in copies:
        copy.wait()


def round_body(pos, q, x0, q1, q2, one_z, one_x, x0_z, four_c):
    one_z[...], one_x[...], x0_z[...] = q2[...], q2[...], x0[...]
    four_c[0], four_c[1], four_c[2], four_c[3] = q[...], q1[...], q2[...], x0[...]


def next_round_body(pos, q3, x2, total, last_x, two_c):
    rows = q3.shape[0]
    last_x[0:rows, :] = q3[...]
    last_x[rows : rows + 16, :] = split_rows(total[:, : total.shape[1] // 3])
    two_c[0], two_c[1] = q3[...], x2[...]


def both_cores(kinds, own, core):
    pieces = [(who, j, own.at[n]) for n, (who, j) in enumerate(kinds)]
    return pieces + [(who + 2, j, core.at[n]) for n, (who, j) in enumerate(kinds)]


def first_spread_body(pos, own, core, out, done, wide, sems):
    place(pos, both_cores(((0, 0), (0, 1), (0, 2), (1, 0)), own, core), out, wide, sems)
    done[...] = jnp.zeros_like(done)


def next_spread_body(pos, own, core, before, out, done, wide, sems):
    place(pos, both_cores(((0, 3), (1, 2)), own, core), out, wide, sems)
    done[...] = jnp.zeros_like(done)


def last_spread_body(pos, own, core, before, out, done, wide, sems):
    rows = own.shape[0] // 2
    pieces = []
    for n, (who, j) in enumerate(((1, 1), (1, 3))):
        pieces.append((who, j, own.at[n * rows : (n + 1) * rows]))
        pieces.append((who + 2, j, core.at[n * rows : (n + 1) * rows]))
    place(pos, pieces, out, wide, sems)
    done[...] = jnp.zeros_like(done)


def spread(body, shape, small, *arrays, alias=False):
    whole = pl.BlockSpec(memory_space=pltpu.VMEM)
    anywhere = pl.BlockSpec(memory_space=pl.ANY)

    def inner(*refs):
        body(position(), *refs)

    return pl.pallas_call(
        inner,
        out_shape=[jax.ShapeDtypeStruct(shape, F32), jax.ShapeDtypeStruct(*small)],
        in_specs=[whole] * (len(arrays) - alias) + [anywhere] * alias,
        out_specs=[anywhere, whole],
        scratch_shapes=[pltpu.VMEM((8, shape[0], 16, shape[2] // 2), F32), pltpu.SemaphoreType.DMA((8,))],
        input_output_aliases={len(arrays) - 1: 0} if alias else {},
        compiler_params=pltpu.CompilerParams(vmem_limit_bytes=20 * MIB),
        cost_estimate=pl.CostEstimate(flops=1, bytes_accessed=1, transcendentals=0),
    )(*arrays)


def whole(x, keep, other):
    first = jnp.where(x == 0, keep, other)
    return jnp.concatenate([first, jnp.where(x == 0, other, keep)], axis=1)


def input_taps(ny, depths, wt, buf, at):
    cells = buf.shape[1] - 2 * ny
    lanes = buf.shape[2] // 3
    acc = jnp.zeros((cells, len(depths) * wt.shape[1]), F32)
    for b in range(3):
        for c in range(3):
            lhs = buf[at, (2 - b) * ny : (2 - b) * ny + cells, c * lanes : (c + 1) * lanes]
            rhs = jnp.concatenate([wt[depth * 9 + b * 3 + c] for depth in depths], axis=0)
            acc = acc + lax.dot_general(lhs, rhs, (((1,), (1,)), ((), ())), preferred_element_type=F32)
    return acc


def near_input_body(ny, pos, kn, on, kf, of, near, near_o, wt, act_n, act_f, out, partial, act, done, buf):
    odd, x = pos[0], pos[6]
    put_plane(buf, 0, whole(x, kn[...], on[...]), ny, True)
    put_plane(buf, 1, whole(x, kf[...], of[...]), ny, True)
    put_plane(buf, 2, whole(x, near[...], near_o[...]), ny, True)
    half = out.shape[1]
    both = input_taps(ny, (1, 2 * odd), wt, buf, 0)
    swapped = input_taps(ny, (2 - 2 * odd, 1), wt, buf, 1)
    out[...] = (both[:, :half] + swapped[:, :half] + input_taps(ny, (2 * odd,), wt, buf, 2)).astype(BF)
    partial[...] = both[:, half:] + swapped[:, half:]
    done[...] = jnp.zeros_like(done)
    act[1 - odd] = act_n[...]
    act[odd] = act_f[...]


def far_input_body(inside, ny, pos, far, far_o, wt, partial, ig_n, out, done, buf):
    odd, x, mine = pos[0], pos[6], pos[2]
    beyond = whole(x, far[...], far_o[...])
    if inside:
        beyond = jnp.where((mine == 0) | (mine == 3), jnp.zeros_like(beyond), beyond)
    put_plane(buf, 0, beyond, ny, True)
    out[odd] = (partial[...] + input_taps(ny, (2 - 2 * odd,), wt, buf, 0)).astype(BF)
    out[1 - odd] = ig_n[...]
    done[...] = jnp.zeros_like(done)


def per_device(volumes, weight, bias, cotangent):
    samples, planes, nx, ny, local_in = volumes.shape
    outputs = weight.shape[4]
    local_out = bias.shape[0]
    plane = nx * ny
    cells = planes * plane
    slabs = lax.axis_size("slab")
    s, z, y = lax.axis_index("slab"), lax.axis_index("dp"), lax.axis_index("chan")
    odd, mine, x = s % 2, s % 4, (s // 2) % 2
    factor = float(samples * cells * slabs * lax.axis_size("dp")) ** -0.5
    padded = plane + 2 * ny
    macs = plane * 27 * local_in * outputs

    def next_pair(value):
        pairs = [(i, i + 1) for i in range(1, slabs - 1, 2)]
        return lax.ppermute(value, "slab", pairs + [(j, i) for i, j in pairs])

    vol = volumes.reshape(planes, plane, local_in)
    w = weight.reshape(3, 9 * local_in, outputs)
    vol_n = jnp.where(odd == 0, vol[1], vol[0])
    vol_f = jnp.where(odd == 0, vol[0], vol[1])
    near, x_f = swap(vol_n, "slab", 1), swap(vol_f, "slab", 2)
    ends = group_ends(vol, slabs)
    wide, thin = ((plane, local_out), F32), ((plane, local_out), BF)
    one = [pltpu.VMEM((1, padded, 3 * local_in), BF)]
    own_n, send_n, kept, held, done_n = vmem_call(
        functools.partial(near_body, ny),
        [wide, thin, ((2, padded, 3 * local_in), BF), (w.shape, BF), ((8, 128), F32)],
        one + [pltpu.SemaphoreType.DMA(())],
        macs,
        vol_n, vol_f, near, w,
    )
    recv_n = swap(send_n, "chan", 1)
    cx_f = swap(held_back(x_f, done_n), "slab", 1)
    beyond = cx_f
    if slabs > 4:
        beyond = jnp.where((mine == 0) | (mine == 3), next_pair(vol_f), beyond)
    own_f, send_f = vmem_call(functools.partial(far_body, ny), [wide, thin], one, macs, beyond, kept, held)
    recv_f = swap(send_f, "chan", 1)

    bias_row, cot = bias.reshape(1, local_out), cotangent.reshape(planes, plane, local_out)
    act_n, g_n, vol_n2 = vmem_call(
        near_gate_body, [thin, thin, thin], [], 0, own_n, recv_n, bias_row, cot, vol_n
    )
    x_n, core_vf = swap(vol_n2, "slab", 2), swap(vol_f, "slab", 1)
    cx_n = swap(x_n, "slab", 1)
    g_ny = swap(g_n, "chan", 1)
    vt = vmem_call(
        volume_body,
        [((4 * planes + 4, 3 * local_in // 2, plane), BF)],
        [],
        0,
        vol_n, vol_f, near, core_vf, x_n, x_f, cx_n, cx_f, ends,
    )[0]
    act_f, g_f = vmem_call(far_gate_body, [thin, thin], [], 0, own_f, recv_f, bias_row, cot, after=(g_n,))
    g_fy = swap(g_f, "chan", 1)
    lanes = 3 * local_out

    def routed(mine_g, other_g):
        keep, send = jnp.where(x == y, mine_g, other_g), jnp.where(x == y, other_g, mine_g)
        return keep, send, swap(send, "slab", 2)

    keep_n, send_n, got_n = routed(g_n, g_ny)
    core_n = swap(keep_n, "slab", 1), swap(got_n, "slab", 1)
    keep_f, send_f, got_f = routed(g_f, g_fy)
    acc_shape = (3, 3 * local_in // 2, lanes)
    core_f = swap(keep_f, "slab", 1)
    sums_of = [(acc_shape, F32), ((8, lanes), F32)]
    four, two = pltpu.VMEM((4, padded, lanes), BF), pltpu.VMEM((2, padded, lanes), BF)
    first = functools.partial(first_kernel_body, ny)
    acc0, total0 = vmem_call(first, sums_of, [four], 2 * macs, vt, keep_n, core_n[0], keep_f, core_f)
    second = functools.partial(second_kernel_body, ny)
    acc0, total0 = vmem_call(second, sums_of, [two], macs, vt, got_n, core_n[1], acc0, total0)
    last_f = swap(held_back(got_f, total0[:, :local_out]), "slab", 1)
    single = pltpu.VMEM((1, padded, lanes), BF)
    acc1, total1 = vmem_call(
        functools.partial(next_kernel_body, 2, ny), sums_of, [single], macs, vt, got_f, acc0, total0
    )
    rows = 9 * local_in // 8
    cut = [((rows, lanes), F32), ((rows, lanes), BF), ((rows, lanes), F32), ((rows, lanes), BF)]
    if slabs == 4:
        keep, s1, s2, s3, total, sent = vmem_call(
            functools.partial(last_kernel_body, ny),
            cut + [((8, lanes), F32), thin],
            [single, pltpu.VMEM(acc_shape, F32)],
            macs,
            vt, last_f, acc1, total1, keep_f,
        )
    else:
        acc, total = vmem_call(
            functools.partial(next_kernel_body, 3, ny), sums_of, [single], macs, vt, last_f, acc1, total1
        )
        bit = 4
        while bit < slabs:
            acc, total = acc + swap(acc, "slab", bit), total + swap(total, "slab", bit)
            bit *= 2
        keep, s1, s2, s3 = vmem_call(cut_body, cut, [], 0, acc)
        sent = keep_f
    r3, r1, total_z2 = swap(s3, "dp", 1), swap(s1, "dp", 1), swap(total, "dp", 2)
    merged, total_a = (s2 + r3.astype(F32)).astype(BF), total + total_z2
    r2 = swap(merged, "dp", 2)

    sent_x = swap(sent, "slab", 2)
    wt = weight.reshape(27, local_in, outputs)
    ig_buf = pltpu.VMEM((3, padded, 3 * outputs), BF)
    ig_n, partial, act, ig_n_done = vmem_call(
        functools.partial(near_input_body, ny),
        [
            ((plane, local_in), BF), ((plane, local_in), F32), ((planes, plane, local_out), BF), ((8, lanes), F32)
        ],
        [ig_buf],
        2 * macs,
        keep_n, send_n, keep_f, send_f, core_n[0], swap(send_n, "slab", 1), wt, act_n, act_f,
        after=(merged, sent_x),
    )
    far_keep = last_f
    far_send = swap(sent_x, "slab", 1)
    if slabs > 4:
        edge = (mine == 0) | (mine == 3)
        far_keep = jnp.where(edge, next_pair(send_f), far_keep)
        far_send = jnp.where(edge, next_pair(keep_f), far_send)
    ig, ig_done = vmem_call(
        functools.partial(far_input_body, slabs == 4, ny),
        [((planes, plane, local_in), BF), ((8, lanes), F32)],
        [pltpu.VMEM((1, padded, 3 * outputs), BF)],
        0,
        far_keep, far_send, wt, partial, ig_n,
    )
    quarter = held_back(((keep + r1.astype(F32) + r2.astype(F32)) * factor).astype(BF), ig_n_done, total_z2)
    total_z1 = swap(total_a, "dp", 1)
    q1, q2, x0 = swap(quarter, "dp", 1), swap(quarter, "dp", 2), swap(quarter, "slab", 2)
    total_b = total_a + total_z1
    out_shape = (27, local_in, outputs)
    token = (8, lanes), F32
    one_z, one_x, x0_z, four_c = vmem_call(
        round_body,
        [(quarter.shape, BF)] * 3 + [((4,) + quarter.shape, BF)],
        [],
        0,
        quarter, x0, q1, q2,
        after=(total_z1, ig_done),
    )
    q3, x2, x1, core = swap(one_z, "dp", 1), swap(one_x, "slab", 2), swap(x0_z, "dp", 1), swap(four_c, "slab", 1)
    out, done = spread(first_spread_body, out_shape, token, four_c, core)
    last_x, two_c = vmem_call(
        next_round_body,
        [((rows + 16, lanes), BF), ((2,) + quarter.shape, BF)],
        [],
        0,
        q3, x2, total_b,
        after=(done,),
    )
    x3, core_b = swap(last_x, "slab", 2), swap(two_c, "slab", 1)
    out, done = spread(next_spread_body, out_shape, token, two_c, core_b, out, alias=True)
    x3 = held_back(x3, done)
    pair_x = jnp.concatenate([x1, x3[:rows]], axis=0)
    core_x = swap(pair_x, "slab", 1)
    weight_grad, _ = spread(last_spread_body, out_shape, token, pair_x, core_x, out, alias=True)
    tail = x3[rows : rows + 1].astype(F32).reshape(3, local_out)
    bias_grad = jnp.where(x == y, total_b[0, :local_out], tail[0] + tail[1] + tail[2]) * factor
    shape = (samples, planes, nx, ny)
    return (
        act.reshape(shape + (local_out,)),
        ig.reshape(shape + (local_in,)),
        weight_grad.reshape(weight.shape),
        bias_grad,
    )


def group_ends(vol, slabs):
    before, after = jnp.zeros_like(vol[0]), jnp.zeros_like(vol[0])
    for group in range(4 if slabs > 4 else 0):
        up = [(i - 1, i + group) for i in range(4, slabs, 4)]
        down = [(i + 4, i + group) for i in range(0, slabs - 4, 4)]
        before = before + lax.ppermute(vol[vol.shape[0] - 1], "slab", up)
        after = after + lax.ppermute(vol[0], "slab", down)
    return jnp.stack([before, after])


def solution(mesh):
    placed = (
        P("dp", "slab", None, None, "chan"),
        P(None, None, None, "chan", None),
        P("chan"),
        P("dp", "slab", None, None, "chan"),
    )
    return jax.shard_map(
        per_device,
        mesh=mesh,
        in_specs=placed,
        out_specs=(
            P("dp", "slab", None, None, "chan"),
            P("dp", "slab", None, None, "chan"),
            P(None, None, None, "chan", None),
            P("chan"),
        ),
        check_vma=False,
    )
```

```python
import functools

import jax
import jax.numpy as jnp
from jax import lax
from jax.experimental import pallas as pl
from jax.experimental.pallas import tpu as pltpu
from jax.sharding import PartitionSpec as P

BF = jnp.bfloat16
F32 = jnp.float32
MIB = 1 << 20


def swap(value, axis, bit):
    return lax.ppermute(value, axis, [(i, i ^ bit) for i in range(lax.axis_size(axis))])


def position():
    s, z, y = lax.axis_index("slab"), lax.axis_index("dp"), lax.axis_index("chan")
    odd = s & 1
    beside = jnp.where((s == 0) | (s == lax.axis_size("slab") - 1), 0, 1)
    return odd, y, s & 3, odd, z, z, (s >> 1) & 1, beside


def vmem_call(body, outs, scratch, flops, *args, after=(), limit=20):
    shapes = [jax.ShapeDtypeStruct(s, d) for s, d in outs]
    count, waited = len(args), len(after)

    def inner(*refs):
        body(position(), *refs[:count], *refs[count + waited :])

    return pl.pallas_call(
        inner,
        out_shape=shapes,
        in_specs=[pl.BlockSpec(memory_space=pltpu.VMEM)] * count + [pl.BlockSpec(memory_space=pl.ANY)] * waited,
        out_specs=[pl.BlockSpec(memory_space=pltpu.VMEM)] * len(shapes),
        scratch_shapes=scratch,
        compiler_params=pltpu.CompilerParams(vmem_limit_bytes=limit * MIB),
        cost_estimate=pl.CostEstimate(flops=4 * flops + 10**9, bytes_accessed=MIB, transcendentals=0),
    )(*args, *after)


def shift_y(value, step, ny):
    rows = value.shape[0]
    y = lax.broadcasted_iota(jnp.int32, value.shape, 0) % ny
    rolled = pltpu.roll(value, (-step) % rows, 0)
    return jnp.where(y == (0 if step < 0 else ny - 1), 0.0, rolled)


def put_plane(buf, at, value, ny, flip):
    cells, lanes = value.shape
    wide = value.astype(F32)
    edge = jnp.zeros((ny, 3 * lanes), BF)
    buf[at, 0:ny, :] = edge
    buf[at, ny + cells : 2 * ny + cells, :] = edge
    for c in range(3):
        step = (1 - c) if flip else (c - 1)
        moved = value if step == 0 else shift_y(wide, step, ny).astype(BF)
        buf[at, ny : ny + cells, c * lanes : (c + 1) * lanes] = moved


def near_body(ny, pos, vol_n, vol_f, plane, w, own, send, kept, held, done, buf, sem):
    copy = pltpu.make_async_copy(w, held, sem)
    copy.start()
    put_plane(kept, 0, vol_n[...], ny, False)
    put_plane(kept, 1, vol_f[...], ny, False)
    put_plane(buf, 0, plane[...], ny, False)
    sums(ny, pos, kept.at[0], kept.at[1], buf.at[0], 2 - 2 * pos[0], w, own, send)
    done[...] = jnp.zeros_like(done)
    copy.wait()


def far_body(ny, pos, beyond, kept, w, own, send, buf):
    odd = pos[0]
    put_plane(buf, 0, jnp.where(pos[7] == 0, 0.0, beyond[...].astype(F32)).astype(BF), ny, False)
    sums(ny, pos, kept.at[1], kept.at[0], buf.at[0], 2 * odd, w, own, send)


def sums(ny, pos, middle, inner, outer, depth, w, own, send):
    cells = own.shape[0]
    y, half = pos[1], own.shape[1]
    total = tap(middle, w, 1, ny, cells) + tap(inner, w, 2 - depth, ny, cells) + tap(outer, w, depth, ny, cells)
    own[...] = jnp.where(y == 0, total[:, :half], total[:, half:])
    send[...] = jnp.where(y == 0, total[:, half:], total[:, :half]).astype(BF)


def tap(field, w, depth, ny, cells):
    lhs = jnp.concatenate([field[b * ny : b * ny + cells, :] for b in range(3)], axis=1)
    return jnp.dot(lhs, w[depth], preferred_element_type=F32)


def gate(pos, plane, own, recv, bias, cot):
    pre = own[...] + recv[...].astype(F32) + bias[...].astype(F32)
    s = 1.0 / (1.0 + jnp.exp(-pre))
    return (pre * s).astype(BF), (cot[plane].astype(F32) * s * (1.0 + pre * (1.0 - s))).astype(BF)


def near_gate_body(pos, own, recv, bias, cot, vol_n, act, grad, vol_out):
    act[...], grad[...] = gate(pos, 1 - pos[0], own, recv, bias, cot)
    vol_out[...] = vol_n[...]


def far_gate_body(pos, own, recv, bias, cot, act, grad):
    act[...], grad[...] = gate(pos, pos[0], own, recv, bias, cot)


def held_back(value, *tokens):
    rows, lanes = value.shape
    ready = functools.reduce(jnp.logical_and, [token == token for token in tokens])
    blocks = value.reshape(rows // 8, 8, lanes)
    return jnp.where(ready[None], blocks, jnp.zeros_like(blocks)).reshape(rows, lanes)


def volume_body(pos, n0, f0, n1, f1, n2, f2, n3, f3, ends, vt):
    lanes = n0.shape[1]
    mine, k, odd = pos[2], pos[3], pos[0]
    keep = lanes // 2

    def put(at, value):
        turned = value.astype(F32).T
        turned = jnp.where(k == 0, turned[:keep], turned[keep:]).astype(BF)
        for a in range(3):
            vt[at + 2 - a, a * keep : (a + 1) * keep, :] = turned

    put(0, ends[0])
    put(9, ends[1])
    for who, (near, far) in enumerate(((n0, f0), (n1, f1), (n2, f2), (n3, f3))):
        own_odd = odd if who in (0, 2) else 1 - odd
        put((mine ^ who) * 2 + (1 - own_odd) + 1, near[...])
        put((mine ^ who) * 2 + own_odd + 1, far[...])


def kernel_terms(ny, pos, vt, grads, buf, acc, before):
    cells, lanes = grads[0][2].shape
    mine, odd = pos[2], pos[0]
    bsum = jnp.zeros((1, lanes), F32)
    where = []
    for n, (far, who, ref) in enumerate(grads):
        own_odd = odd if who in (0, 2) else 1 - odd
        where.append((mine ^ who) * 2 + (own_odd if far else 1 - own_odd) + 2)
        value = ref[...]
        put_plane(buf, n, value, ny, True)
        bsum = bsum + jnp.sum(value.astype(F32), axis=0, keepdims=True)
    lhs = jnp.concatenate([vt[at] for at in where], axis=1)
    for b in range(3):
        rhs = [buf[n, (2 - b) * ny : (2 - b) * ny + cells, :] for n in range(len(grads))]
        summed = jnp.dot(lhs, jnp.concatenate(rhs, axis=0), preferred_element_type=F32)
        acc[b] = summed if before is None else summed + before[b]
    return bsum


def first_kernel_body(ny, pos, vt, g0, g1, f0, f1, acc, total, buf):
    grads = ((0, 0, g0), (0, 1, g1), (1, 0, f0), (1, 1, f1))
    bsum = kernel_terms(ny, pos, vt, grads, buf, acc, None)
    total[...] = jnp.broadcast_to(jnp.concatenate([bsum] * 3, axis=1), total.shape)


def second_kernel_body(ny, pos, vt, g2, g3, acc0, total0, acc, total, buf):
    bsum = kernel_terms(ny, pos, vt, ((0, 2, g2), (0, 3, g3)), buf, acc, acc0)
    total[...] = total0[...] + jnp.concatenate([bsum] * 3, axis=1)


def next_kernel_body(who, ny, pos, vt, f, acc0, total0, acc, total, buf):
    bsum = kernel_terms(ny, pos, vt, ((1, who, f),), buf, acc, acc0)
    total[...] = total0[...] + jnp.concatenate([bsum] * 3, axis=1)


def last_kernel_body(ny, pos, vt, f3, acc0, total0, kf, keep, s1, s2, s3, total, sent, buf, acc):
    sent[...] = kf[...]
    next_kernel_body(3, ny, pos, vt, f3, acc0, total0, acc, total, buf)
    cut_body(pos, acc, keep, s1, s2, s3)


def cut_body(pos, acc, keep, s1, s2, s3):
    part = keep.shape[0] // 9
    mine = pos[4]
    for b in range(3):
        for a in range(3):
            rows = slice((3 * b + a) * part, (3 * b + a + 1) * part)
            for who, ref in ((0, keep), (1, s1), (2, s2), (3, s3)):
                at = pl.multiple_of((4 * a + (mine ^ who)) * part, part)
                ref[rows, :] = acc[b, pl.ds(at, part), :].astype(ref.dtype)


def split_rows(total):
    value = jnp.broadcast_to(total[0:1, :], (16, total.shape[1]))
    high = value.astype(BF)
    rest = value - high.astype(F32)
    mid = rest.astype(BF)
    low = (rest - mid.astype(F32)).astype(BF)
    return jnp.concatenate([high, mid, low], axis=1)


def place(pos, pieces, out, wide, sems):
    x, k, mine = pos[6], pos[3], pos[4]
    half = out.shape[2] // 2
    copies = []
    for n, (who, j, piece) in enumerate(pieces):
        for b in range(3):
            for a in range(3):
                for c in range(3):
                    rows = slice((3 * b + a) * 16, (3 * b + a + 1) * 16)
                    wide[n, (a * 3 + b) * 3 + c] = piece[rows, c * half : (c + 1) * half].astype(F32)
        row = pl.multiple_of((k ^ (who >> 1)) * 64 + (mine ^ j) * 16, 16)
        lane = pl.multiple_of((x ^ (who & 1)) * half, half)
        copy = pltpu.make_async_copy(wide.at[n], out.at[:, pl.ds(row, 16), pl.ds(lane, half)], sems.at[n])
        copy.start()
        copies.append(copy)
    for copy in copies:
        copy.wait()


def round_body(pos, q, x0, q1, q2, one_z, one_x, x0_z, four_c):
    one_z[...], one_x[...], x0_z[...] = q2[...], q2[...], x0[...]
    four_c[0], four_c[1], four_c[2], four_c[3] = q[...], q1[...], q2[...], x0[...]


def next_round_body(pos, core, q3, x2, total, last_x, two_c):
    del core
    rows = q3.shape[0]
    last_x[0:rows, :] = q3[...]
    last_x[rows : rows + 16, :] = split_rows(total[:, : total.shape[1] // 3])
    two_c[0], two_c[1] = q3[...], x2[...]


FIRST, NEXT, LAST = ((0, 0), (0, 1), (0, 2), (1, 0)), ((0, 3), (1, 2)), ((1, 1), (1, 3))


def stacked(kinds, own, core):
    pieces = [(who, j, own.at[n]) for n, (who, j) in enumerate(kinds)] if own is not None else []
    return pieces + ([(who + 2, j, core.at[n]) for n, (who, j) in enumerate(kinds)] if core is not None else [])


def first_spread_body(pos, own, core, own_b, out, done, wide, sems):
    place(pos, stacked(FIRST, own, core) + stacked(NEXT, own_b, None), out, wide, sems)
    done[...] = jnp.zeros_like(done)


def last_spread_body(pos, own, core, core_b, before, out, wide, sems):
    rows = own.shape[0] // 2
    pieces = []
    for n, (who, j) in enumerate(LAST):
        pieces.append((who, j, own.at[n * rows : (n + 1) * rows]))
        pieces.append((who + 2, j, core.at[n * rows : (n + 1) * rows]))
    place(pos, pieces + stacked(NEXT, None, core_b), out, wide, sems)


def spread(body, shape, small, *arrays, alias=False):
    whole = pl.BlockSpec(memory_space=pltpu.VMEM)
    anywhere = pl.BlockSpec(memory_space=pl.ANY)

    def inner(*refs):
        body(position(), *refs)

    return pl.pallas_call(
        inner,
        out_shape=[jax.ShapeDtypeStruct(shape, F32)] + [jax.ShapeDtypeStruct(*one) for one in small],
        in_specs=[whole] * (len(arrays) - alias) + [anywhere] * alias,
        out_specs=[anywhere] + [whole] * len(small),
        scratch_shapes=[pltpu.VMEM((10, shape[0], 16, shape[2] // 2), F32), pltpu.SemaphoreType.DMA((10,))],
        input_output_aliases={len(arrays) - 1: 0} if alias else {},
        compiler_params=pltpu.CompilerParams(vmem_limit_bytes=20 * MIB),
        cost_estimate=pl.CostEstimate(flops=1, bytes_accessed=1, transcendentals=0),
    )(*arrays)


def whole(x, keep, other):
    first = jnp.where(x == 0, keep, other)
    return jnp.concatenate([first, jnp.where(x == 0, other, keep)], axis=1)


def input_taps(ny, depths, wt, buf, at):
    cells = buf.shape[1] - 2 * ny
    lanes = buf.shape[2] // 3
    acc = jnp.zeros((cells, len(depths) * wt.shape[1]), F32)
    for b in range(3):
        for c in range(3):
            lhs = buf[at, (2 - b) * ny : (2 - b) * ny + cells, c * lanes : (c + 1) * lanes]
            rhs = jnp.concatenate([wt[depth * 9 + b * 3 + c] for depth in depths], axis=0)
            acc = acc + lax.dot_general(lhs, rhs, (((1,), (1,)), ((), ())), preferred_element_type=F32)
    return acc


def near_input_body(ny, pos, kn, on, kf, of, near, near_o, wt, act_n, act_f, out, partial, act, done, buf):
    odd, x = pos[0], pos[6]
    put_plane(buf, 0, whole(x, kn[...], on[...]), ny, True)
    put_plane(buf, 1, whole(x, kf[...], of[...]), ny, True)
    put_plane(buf, 2, whole(x, near[...], near_o[...]), ny, True)
    half = out.shape[1]
    both = input_taps(ny, (1, 2 * odd), wt, buf, 0)
    swapped = input_taps(ny, (2 - 2 * odd, 1), wt, buf, 1)
    out[...] = (both[:, :half] + swapped[:, :half] + input_taps(ny, (2 * odd,), wt, buf, 2)).astype(BF)
    partial[...] = both[:, half:] + swapped[:, half:]
    done[...] = jnp.zeros_like(done)
    act[1 - odd] = act_n[...]
    act[odd] = act_f[...]


def far_input_body(inside, ny, pos, far, far_o, wt, partial, ig_n, out, done, buf):
    odd, x, mine = pos[0], pos[6], pos[2]
    beyond = whole(x, far[...], far_o[...])
    if inside:
        beyond = jnp.where((mine == 0) | (mine == 3), jnp.zeros_like(beyond), beyond)
    put_plane(buf, 0, beyond, ny, True)
    out[odd] = (partial[...] + input_taps(ny, (2 - 2 * odd,), wt, buf, 0)).astype(BF)
    out[1 - odd] = ig_n[...]
    done[...] = jnp.zeros_like(done)


def per_device(volumes, weight, bias, cotangent):
    samples, planes, nx, ny, local_in = volumes.shape
    outputs = weight.shape[4]
    local_out = bias.shape[0]
    plane = nx * ny
    cells = planes * plane
    slabs = lax.axis_size("slab")
    s, z, y = lax.axis_index("slab"), lax.axis_index("dp"), lax.axis_index("chan")
    odd, mine, x = s % 2, s % 4, (s // 2) % 2
    factor = float(samples * cells * slabs * lax.axis_size("dp")) ** -0.5
    padded = plane + 2 * ny
    macs = plane * 27 * local_in * outputs

    def next_pair(value):
        pairs = [(i, i + 1) for i in range(1, slabs - 1, 2)]
        return lax.ppermute(value, "slab", pairs + [(j, i) for i, j in pairs])

    vol = volumes.reshape(planes, plane, local_in)
    w = weight.reshape(3, 9 * local_in, outputs)
    vol_n = jnp.where(odd == 0, vol[1], vol[0])
    vol_f = jnp.where(odd == 0, vol[0], vol[1])
    near, x_f = swap(vol_n, "slab", 1), swap(vol_f, "slab", 2)
    ends = group_ends(vol, slabs)
    wide, thin = ((plane, local_out), F32), ((plane, local_out), BF)
    one = [pltpu.VMEM((1, padded, 3 * local_in), BF)]
    own_n, send_n, kept, held, done_n = vmem_call(
        functools.partial(near_body, ny),
        [wide, thin, ((2, padded, 3 * local_in), BF), (w.shape, BF), ((8, 128), F32)],
        one + [pltpu.SemaphoreType.DMA(())],
        macs,
        vol_n, vol_f, near, w,
    )
    recv_n = swap(send_n, "chan", 1)
    cx_f = swap(held_back(x_f, done_n), "slab", 1)
    beyond = cx_f
    if slabs > 4:
        beyond = jnp.where((mine == 0) | (mine == 3), next_pair(vol_f), beyond)
    own_f, send_f = vmem_call(functools.partial(far_body, ny), [wide, thin], one, macs, beyond, kept, held)
    recv_f = swap(send_f, "chan", 1)

    bias_row, cot = bias.reshape(1, local_out), cotangent.reshape(planes, plane, local_out)
    act_n, g_n, vol_n2 = vmem_call(
        near_gate_body, [thin, thin, thin], [], 0, own_n, recv_n, bias_row, cot, vol_n
    )
    x_n, core_vf = swap(vol_n2, "slab", 2), swap(vol_f, "slab", 1)
    cx_n = swap(x_n, "slab", 1)
    g_ny = swap(g_n, "chan", 1)
    vt = vmem_call(
        volume_body,
        [((4 * planes + 4, 3 * local_in // 2, plane), BF)],
        [],
        0,
        vol_n, vol_f, near, core_vf, x_n, x_f, cx_n, cx_f, ends,
    )[0]
    act_f, g_f = vmem_call(far_gate_body, [thin, thin], [], 0, own_f, recv_f, bias_row, cot, after=(g_n,))
    g_fy = swap(g_f, "chan", 1)
    lanes = 3 * local_out

    def routed(mine_g, other_g):
        keep, send = jnp.where(x == y, mine_g, other_g), jnp.where(x == y, other_g, mine_g)
        return keep, send, swap(send, "slab", 2)

    keep_n, send_n, got_n = routed(g_n, g_ny)
    core_n = swap(keep_n, "slab", 1), swap(got_n, "slab", 1)
    keep_f, send_f, got_f = routed(g_f, g_fy)
    acc_shape = (3, 3 * local_in // 2, lanes)
    core_f = swap(keep_f, "slab", 1)
    sums_of = [(acc_shape, F32), ((8, lanes), F32)]
    four, two = pltpu.VMEM((4, padded, lanes), BF), pltpu.VMEM((2, padded, lanes), BF)
    first = functools.partial(first_kernel_body, ny)
    acc0, total0 = vmem_call(first, sums_of, [four], 2 * macs, vt, keep_n, core_n[0], keep_f, core_f)
    second = functools.partial(second_kernel_body, ny)
    acc0, total0 = vmem_call(second, sums_of, [two], macs, vt, got_n, core_n[1], acc0, total0)
    last_f = swap(held_back(got_f, total0[:, :local_out]), "slab", 1)
    single = pltpu.VMEM((1, padded, lanes), BF)
    acc1, total1 = vmem_call(
        functools.partial(next_kernel_body, 2, ny), sums_of, [single], macs, vt, got_f, acc0, total0
    )
    rows = 9 * local_in // 8
    cut = [((rows, lanes), F32), ((rows, lanes), BF), ((rows, lanes), F32), ((rows, lanes), BF)]
    if slabs == 4:
        keep, s1, s2, s3, total, sent = vmem_call(
            functools.partial(last_kernel_body, ny),
            cut + [((8, lanes), F32), thin],
            [single, pltpu.VMEM(acc_shape, F32)],
            macs,
            vt, last_f, acc1, total1, keep_f,
        )
    else:
        acc, total = vmem_call(
            functools.partial(next_kernel_body, 3, ny), sums_of, [single], macs, vt, last_f, acc1, total1
        )
        bit = 4
        while bit < slabs:
            acc, total = acc + swap(acc, "slab", bit), total + swap(total, "slab", bit)
            bit *= 2
        keep, s1, s2, s3 = vmem_call(cut_body, cut, [], 0, acc)
        sent = keep_f
    r3, r1, total_z2 = swap(s3, "dp", 1), swap(s1, "dp", 1), swap(total, "dp", 2)
    merged, total_a = (s2 + r3.astype(F32)).astype(BF), total + total_z2
    r2 = swap(merged, "dp", 2)

    sent_x = swap(sent, "slab", 2)
    wt = weight.reshape(27, local_in, outputs)
    ig_buf = pltpu.VMEM((3, padded, 3 * outputs), BF)
    ig_n, partial, act, ig_n_done = vmem_call(
        functools.partial(near_input_body, ny),
        [
            ((plane, local_in), BF), ((plane, local_in), F32), ((planes, plane, local_out), BF), ((8, lanes), F32)
        ],
        [ig_buf],
        2 * macs,
        keep_n, send_n, keep_f, send_f, core_n[0], swap(send_n, "slab", 1), wt, act_n, act_f,
        after=(merged, sent_x),
    )
    far_keep = last_f
    far_send = swap(sent_x, "slab", 1)
    if slabs > 4:
        edge = (mine == 0) | (mine == 3)
        far_keep = jnp.where(edge, next_pair(send_f), far_keep)
        far_send = jnp.where(edge, next_pair(keep_f), far_send)
    ig, ig_done = vmem_call(
        functools.partial(far_input_body, slabs == 4, ny),
        [((planes, plane, local_in), BF), ((8, lanes), F32)],
        [pltpu.VMEM((1, padded, 3 * outputs), BF)],
        0,
        far_keep, far_send, wt, partial, ig_n,
    )
    quarter = held_back(((keep + r1.astype(F32) + r2.astype(F32)) * factor).astype(BF), ig_n_done, total_z2)
    total_z1 = swap(total_a, "dp", 1)
    q1, q2, x0 = swap(quarter, "dp", 1), swap(quarter, "dp", 2), swap(quarter, "slab", 2)
    total_b = total_a + total_z1
    out_shape = (27, local_in, outputs)
    token = (((8, lanes), F32),)
    one_z, one_x, x0_z, four_c = vmem_call(
        round_body,
        [(quarter.shape, BF)] * 3 + [((4,) + quarter.shape, BF)],
        [],
        0,
        quarter, x0, q1, q2,
        after=(total_z1, ig_done),
    )
    q3, x2, x1, core = swap(one_z, "dp", 1), swap(one_x, "slab", 2), swap(x0_z, "dp", 1), swap(four_c, "slab", 1)
    last_x, two_c = vmem_call(
        next_round_body,
        [((rows + 16, lanes), BF), ((2,) + quarter.shape, BF)],
        [],
        0,
        core, q3, x2, total_b,
    )
    x3, core_b = swap(last_x, "slab", 2), swap(two_c, "slab", 1)
    out, done = spread(first_spread_body, out_shape, token, four_c, core, two_c)
    x3 = held_back(x3, done)
    pair_x = jnp.concatenate([x1, x3[:rows]], axis=0)
    core_x = swap(pair_x, "slab", 1)
    weight_grad = spread(last_spread_body, out_shape, (), pair_x, core_x, core_b, out, alias=True)[0]
    tail = x3[rows : rows + 1].astype(F32).reshape(3, local_out)
    bias_grad = jnp.where(x == y, total_b[0, :local_out], tail[0] + tail[1] + tail[2]) * factor
    shape = (samples, planes, nx, ny)
    return (
        act.reshape(shape + (local_out,)),
        ig.reshape(shape + (local_in,)),
        weight_grad.reshape(weight.shape),
        bias_grad,
    )


def group_ends(vol, slabs):
    before, after = jnp.zeros_like(vol[0]), jnp.zeros_like(vol[0])
    for group in range(4 if slabs > 4 else 0):
        up = [(i - 1, i + group) for i in range(4, slabs, 4)]
        down = [(i + 4, i + group) for i in range(0, slabs - 4, 4)]
        before = before + lax.ppermute(vol[vol.shape[0] - 1], "slab", up)
        after = after + lax.ppermute(vol[0], "slab", down)
    return jnp.stack([before, after])


def solution(mesh):
    placed = (
        P("dp", "slab", None, None, "chan"),
        P(None, None, None, "chan", None),
        P("chan"),
        P("dp", "slab", None, None, "chan"),
    )
    return jax.shard_map(
        per_device,
        mesh=mesh,
        in_specs=placed,
        out_specs=(
            P("dp", "slab", None, None, "chan"),
            P("dp", "slab", None, None, "chan"),
            P(None, None, None, "chan", None),
            P("chan"),
        ),
        check_vma=False,
    )
```

```python
import functools

import jax
import jax.numpy as jnp
from jax import lax
from jax.experimental import pallas as pl
from jax.experimental.pallas import tpu as pltpu
from jax.sharding import PartitionSpec as P

BF = jnp.bfloat16
F32 = jnp.float32
MIB = 1 << 20


def swap(value, axis, bit):
    return lax.ppermute(value, axis, [(i, i ^ bit) for i in range(lax.axis_size(axis))])


def position():
    s, z, y = lax.axis_index("slab"), lax.axis_index("dp"), lax.axis_index("chan")
    odd = s & 1
    beside = jnp.where((s == 0) | (s == lax.axis_size("slab") - 1), 0, 1)
    return odd, y, s & 3, odd, z, z, (s >> 1) & 1, beside


def vmem_call(body, outs, scratch, flops, *args, after=(), limit=20):
    shapes = [jax.ShapeDtypeStruct(s, d) for s, d in outs]
    count, waited = len(args), len(after)

    def inner(*refs):
        body(position(), *refs[:count], *refs[count + waited :])

    return pl.pallas_call(
        inner,
        out_shape=shapes,
        in_specs=[pl.BlockSpec(memory_space=pltpu.VMEM)] * count + [pl.BlockSpec(memory_space=pl.ANY)] * waited,
        out_specs=[pl.BlockSpec(memory_space=pltpu.VMEM)] * len(shapes),
        scratch_shapes=scratch,
        compiler_params=pltpu.CompilerParams(vmem_limit_bytes=limit * MIB),
        cost_estimate=pl.CostEstimate(flops=4 * flops + 10**9, bytes_accessed=MIB, transcendentals=0),
    )(*args, *after)


def shift_y(value, step, ny):
    rows = value.shape[0]
    y = lax.broadcasted_iota(jnp.int32, value.shape, 0) % ny
    rolled = pltpu.roll(value, (-step) % rows, 0)
    return jnp.where(y == (0 if step < 0 else ny - 1), 0.0, rolled)


def put_plane(buf, at, value, ny, flip):
    cells, lanes = value.shape
    wide = value.astype(F32)
    edge = jnp.zeros((ny, 3 * lanes), BF)
    buf[at, 0:ny, :] = edge
    buf[at, ny + cells : 2 * ny + cells, :] = edge
    for c in range(3):
        step = (1 - c) if flip else (c - 1)
        moved = value if step == 0 else shift_y(wide, step, ny).astype(BF)
        buf[at, ny : ny + cells, c * lanes : (c + 1) * lanes] = moved


def near_body(ny, pos, vol_n, vol_f, plane, w, own, send, kept, held, done, buf, sem):
    copy = pltpu.make_async_copy(w, held, sem)
    copy.start()
    put_plane(kept, 0, vol_n[...], ny, False)
    put_plane(kept, 1, vol_f[...], ny, False)
    put_plane(buf, 0, plane[...], ny, False)
    sums(ny, pos, kept.at[0], kept.at[1], buf.at[0], 2 - 2 * pos[0], w, own, send)
    done[...] = jnp.zeros_like(done)
    copy.wait()


def far_body(ny, pos, beyond, kept, w, own, send, buf):
    odd = pos[0]
    put_plane(buf, 0, jnp.where(pos[7] == 0, 0.0, beyond[...].astype(F32)).astype(BF), ny, False)
    sums(ny, pos, kept.at[1], kept.at[0], buf.at[0], 2 * odd, w, own, send)


def sums(ny, pos, middle, inner, outer, depth, w, own, send):
    cells = own.shape[0]
    y, half = pos[1], own.shape[1]
    total = tap(middle, w, 1, ny, cells) + tap(inner, w, 2 - depth, ny, cells) + tap(outer, w, depth, ny, cells)
    own[...] = jnp.where(y == 0, total[:, :half], total[:, half:])
    send[...] = jnp.where(y == 0, total[:, half:], total[:, :half]).astype(BF)


def tap(field, w, depth, ny, cells):
    lhs = jnp.concatenate([field[b * ny : b * ny + cells, :] for b in range(3)], axis=1)
    return jnp.dot(lhs, w[depth], preferred_element_type=F32)


def gate(pos, plane, own, recv, bias, cot):
    pre = own[...] + recv[...].astype(F32) + bias[...].astype(F32)
    s = 1.0 / (1.0 + jnp.exp(-pre))
    return (pre * s).astype(BF), (cot[plane].astype(F32) * s * (1.0 + pre * (1.0 - s))).astype(BF)


def near_gate_body(pos, own, recv, bias, cot, vol_n, act, grad, vol_out):
    act[...], grad[...] = gate(pos, 1 - pos[0], own, recv, bias, cot)
    vol_out[...] = vol_n[...]


def far_gate_body(pos, own, recv, bias, cot, act, grad):
    act[...], grad[...] = gate(pos, pos[0], own, recv, bias, cot)


def held_back(value, *tokens):
    rows, lanes = value.shape
    ready = functools.reduce(jnp.logical_and, [token == token for token in tokens])
    blocks = value.reshape(rows // 8, 8, lanes)
    return jnp.where(ready[None], blocks, jnp.zeros_like(blocks)).reshape(rows, lanes)


def volume_body(pos, n0, f0, n1, f1, n2, f2, n3, f3, ends, vt):
    lanes = n0.shape[1]
    mine, k, odd = pos[2], pos[3], pos[0]
    keep = lanes // 2

    def put(at, value):
        turned = value.astype(F32).T
        turned = jnp.where(k == 0, turned[:keep], turned[keep:]).astype(BF)
        for a in range(3):
            vt[at + 2 - a, a * keep : (a + 1) * keep, :] = turned

    put(0, ends[0])
    put(9, ends[1])
    for who, (near, far) in enumerate(((n0, f0), (n1, f1), (n2, f2), (n3, f3))):
        own_odd = odd if who in (0, 2) else 1 - odd
        put((mine ^ who) * 2 + (1 - own_odd) + 1, near[...])
        put((mine ^ who) * 2 + own_odd + 1, far[...])


def kernel_terms(ny, pos, vt, grads, buf, acc, before):
    cells, lanes = grads[0][2].shape
    mine, odd = pos[2], pos[0]
    bsum = jnp.zeros((1, lanes), F32)
    where = []
    for n, (far, who, ref) in enumerate(grads):
        own_odd = odd if who in (0, 2) else 1 - odd
        where.append((mine ^ who) * 2 + (own_odd if far else 1 - own_odd) + 2)
        value = ref[...]
        put_plane(buf, n, value, ny, True)
        bsum = bsum + jnp.sum(value.astype(F32), axis=0, keepdims=True)
    lhs = jnp.concatenate([vt[at] for at in where], axis=1)
    for b in range(3):
        rhs = [buf[n, (2 - b) * ny : (2 - b) * ny + cells, :] for n in range(len(grads))]
        summed = jnp.dot(lhs, jnp.concatenate(rhs, axis=0), preferred_element_type=F32)
        acc[b] = summed if before is None else summed + before[b]
    return bsum


def first_kernel_body(ny, pos, vt, g0, g1, f0, f1, acc, total, buf):
    grads = ((0, 0, g0), (0, 1, g1), (1, 0, f0), (1, 1, f1))
    bsum = kernel_terms(ny, pos, vt, grads, buf, acc, None)
    total[...] = jnp.broadcast_to(jnp.concatenate([bsum] * 3, axis=1), total.shape)


def second_kernel_body(ny, pos, vt, g2, g3, acc0, total0, acc, total, buf):
    bsum = kernel_terms(ny, pos, vt, ((0, 2, g2), (0, 3, g3)), buf, acc, acc0)
    total[...] = total0[...] + jnp.concatenate([bsum] * 3, axis=1)


def next_kernel_body(who, ny, pos, vt, f, acc0, total0, acc, total, buf):
    bsum = kernel_terms(ny, pos, vt, ((1, who, f),), buf, acc, acc0)
    total[...] = total0[...] + jnp.concatenate([bsum] * 3, axis=1)


def last_kernel_body(ny, pos, vt, f3, acc0, total0, kf, keep, s1, s2, s3, total, sent, buf, acc):
    sent[...] = kf[...]
    next_kernel_body(3, ny, pos, vt, f3, acc0, total0, acc, total, buf)
    cut_body(pos, acc, keep, s1, s2, s3)


def cut_body(pos, acc, keep, s1, s2, s3):
    part = keep.shape[0] // 9
    mine = pos[4]
    for b in range(3):
        for a in range(3):
            rows = slice((3 * b + a) * part, (3 * b + a + 1) * part)
            for who, ref in ((0, keep), (1, s1), (2, s2), (3, s3)):
                at = pl.multiple_of((4 * a + (mine ^ who)) * part, part)
                ref[rows, :] = acc[b, pl.ds(at, part), :].astype(ref.dtype)


def split_rows(total):
    value = jnp.broadcast_to(total[0:1, :], (16, total.shape[1]))
    high = value.astype(BF)
    rest = value - high.astype(F32)
    mid = rest.astype(BF)
    low = (rest - mid.astype(F32)).astype(BF)
    return jnp.concatenate([high, mid, low], axis=1)


def place(pos, pieces, out, wide, sems):
    x, k, mine = pos[6], pos[3], pos[4]
    half = out.shape[2] // 2
    copies = []
    for n, (who, j, piece) in enumerate(pieces):
        for b in range(3):
            for a in range(3):
                for c in range(3):
                    rows = slice((3 * b + a) * 16, (3 * b + a + 1) * 16)
                    wide[n, (a * 3 + b) * 3 + c] = piece[rows, c * half : (c + 1) * half].astype(F32)
        row = pl.multiple_of((k ^ (who >> 1)) * 64 + (mine ^ j) * 16, 16)
        lane = pl.multiple_of((x ^ (who & 1)) * half, half)
        copy = pltpu.make_async_copy(wide.at[n], out.at[:, pl.ds(row, 16), pl.ds(lane, half)], sems.at[n])
        copy.start()
        copies.append(copy)
    for copy in copies:
        copy.wait()


def round_body(pos, q, x0, q1, q2, one_z, one_x, x0_z, four_c):
    one_z[...], one_x[...], x0_z[...] = q2[...], q2[...], x0[...]
    four_c[0], four_c[1], four_c[2], four_c[3] = q[...], q1[...], q2[...], x0[...]


def next_round_body(pos, core, q3, x2, total, last_x, two_c):
    del core
    rows = q3.shape[0]
    last_x[0:rows, :] = q3[...]
    last_x[rows : rows + 16, :] = split_rows(total[:, : total.shape[1] // 3])
    two_c[0], two_c[1] = q3[...], x2[...]


FIRST, NEXT, LAST = ((0, 0), (0, 1), (0, 2), (1, 0)), ((0, 3), (1, 2)), ((1, 1), (1, 3))


def stacked(kinds, own, core):
    pieces = [(who, j, own.at[n]) for n, (who, j) in enumerate(kinds)] if own is not None else []
    return pieces + ([(who + 2, j, core.at[n]) for n, (who, j) in enumerate(kinds)] if core is not None else [])


def first_spread_body(pos, own, core, own_b, out, done, wide, sems):
    place(pos, stacked(FIRST, own, core) + stacked(NEXT, own_b, None), out, wide, sems)
    done[...] = jnp.zeros_like(done)


def last_spread_body(pos, own, core, core_b, before, out, wide, sems):
    rows = own.shape[0] // 2
    pieces = []
    for n, (who, j) in enumerate(LAST):
        pieces.append((who, j, own.at[n * rows : (n + 1) * rows]))
        pieces.append((who + 2, j, core.at[n * rows : (n + 1) * rows]))
    place(pos, pieces + stacked(NEXT, None, core_b), out, wide, sems)


def spread(body, shape, small, *arrays, alias=False):
    whole = pl.BlockSpec(memory_space=pltpu.VMEM)
    anywhere = pl.BlockSpec(memory_space=pl.ANY)

    def inner(*refs):
        body(position(), *refs)

    return pl.pallas_call(
        inner,
        out_shape=[jax.ShapeDtypeStruct(shape, F32)] + [jax.ShapeDtypeStruct(*one) for one in small],
        in_specs=[whole] * (len(arrays) - alias) + [anywhere] * alias,
        out_specs=[anywhere] + [whole] * len(small),
        scratch_shapes=[pltpu.VMEM((10, shape[0], 16, shape[2] // 2), F32), pltpu.SemaphoreType.DMA((10,))],
        input_output_aliases={len(arrays) - 1: 0} if alias else {},
        compiler_params=pltpu.CompilerParams(vmem_limit_bytes=20 * MIB),
        cost_estimate=pl.CostEstimate(flops=1, bytes_accessed=1, transcendentals=0),
    )(*arrays)


def whole(x, keep, other):
    first = jnp.where(x == 0, keep, other)
    return jnp.concatenate([first, jnp.where(x == 0, other, keep)], axis=1)


def input_taps(ny, depths, wt, buf, at):
    cells = buf.shape[1] - 2 * ny
    lanes = buf.shape[2] // 3
    acc = jnp.zeros((cells, len(depths) * wt.shape[1]), F32)
    for b in range(3):
        for c in range(3):
            lhs = buf[at, (2 - b) * ny : (2 - b) * ny + cells, c * lanes : (c + 1) * lanes]
            rhs = jnp.concatenate([wt[depth * 9 + b * 3 + c] for depth in depths], axis=0)
            acc = acc + lax.dot_general(lhs, rhs, (((1,), (1,)), ((), ())), preferred_element_type=F32)
    return acc


def near_input_body(ny, pos, kn, on, kf, of, near, near_o, wt, act_n, act_f, out, partial, act, done, buf):
    odd, x = pos[0], pos[6]
    put_plane(buf, 0, whole(x, kn[...], on[...]), ny, True)
    put_plane(buf, 1, whole(x, kf[...], of[...]), ny, True)
    put_plane(buf, 2, whole(x, near[...], near_o[...]), ny, True)
    half = out.shape[1]
    both = input_taps(ny, (1, 2 * odd), wt, buf, 0)
    swapped = input_taps(ny, (2 - 2 * odd, 1), wt, buf, 1)
    out[...] = (both[:, :half] + swapped[:, :half] + input_taps(ny, (2 * odd,), wt, buf, 2)).astype(BF)
    partial[...] = both[:, half:] + swapped[:, half:]
    done[...] = jnp.zeros_like(done)
    act[1 - odd] = act_n[...]
    act[odd] = act_f[...]


def far_input_body(inside, ny, pos, far, far_o, wt, partial, ig_n, out, done, buf):
    odd, x, mine = pos[0], pos[6], pos[2]
    beyond = whole(x, far[...], far_o[...])
    if inside:
        beyond = jnp.where((mine == 0) | (mine == 3), jnp.zeros_like(beyond), beyond)
    put_plane(buf, 0, beyond, ny, True)
    out[odd] = (partial[...] + input_taps(ny, (2 - 2 * odd,), wt, buf, 0)).astype(BF)
    out[1 - odd] = ig_n[...]
    done[...] = jnp.zeros_like(done)


def per_device(volumes, weight, bias, cotangent):
    samples, planes, nx, ny, local_in = volumes.shape
    outputs = weight.shape[4]
    local_out = bias.shape[0]
    plane = nx * ny
    cells = planes * plane
    slabs = lax.axis_size("slab")
    s, z, y = lax.axis_index("slab"), lax.axis_index("dp"), lax.axis_index("chan")
    odd, mine, x = s % 2, s % 4, (s // 2) % 2
    factor = float(samples * cells * slabs * lax.axis_size("dp")) ** -0.5
    padded = plane + 2 * ny
    macs = plane * 27 * local_in * outputs

    def next_pair(value):
        pairs = [(i, i + 1) for i in range(1, slabs - 1, 2)]
        return lax.ppermute(value, "slab", pairs + [(j, i) for i, j in pairs])

    vol = volumes.reshape(planes, plane, local_in)
    w = weight.reshape(3, 9 * local_in, outputs)
    vol_n = jnp.where(odd == 0, vol[1], vol[0])
    vol_f = jnp.where(odd == 0, vol[0], vol[1])
    near, x_f = swap(vol_n, "slab", 1), swap(vol_f, "slab", 2)
    ends = group_ends(vol, slabs)
    wide, thin = ((plane, local_out), F32), ((plane, local_out), BF)
    one = [pltpu.VMEM((1, padded, 3 * local_in), BF)]
    own_n, send_n, kept, held, done_n = vmem_call(
        functools.partial(near_body, ny),
        [wide, thin, ((2, padded, 3 * local_in), BF), (w.shape, BF), ((8, 128), F32)],
        one + [pltpu.SemaphoreType.DMA(())],
        macs,
        vol_n, vol_f, near, w,
    )
    recv_n = swap(send_n, "chan", 1)
    cx_f = swap(held_back(x_f, done_n), "slab", 1)
    beyond = cx_f
    if slabs > 4:
        beyond = jnp.where((mine == 0) | (mine == 3), next_pair(vol_f), beyond)
    own_f, send_f = vmem_call(functools.partial(far_body, ny), [wide, thin], one, macs, beyond, kept, held)
    recv_f = swap(send_f, "chan", 1)

    bias_row, cot = bias.reshape(1, local_out), cotangent.reshape(planes, plane, local_out)
    act_n, g_n, vol_n2 = vmem_call(
        near_gate_body, [thin, thin, thin], [], 0, own_n, recv_n, bias_row, cot, vol_n
    )
    x_n, core_vf = swap(vol_n2, "slab", 2), swap(vol_f, "slab", 1)
    cx_n = swap(x_n, "slab", 1)
    g_ny = swap(g_n, "chan", 1)
    vt = vmem_call(
        volume_body,
        [((4 * planes + 4, 3 * local_in // 2, plane), BF)],
        [],
        macs // 2,
        vol_n, vol_f, near, core_vf, x_n, x_f, cx_n, cx_f, ends,
    )[0]
    act_f, g_f = vmem_call(far_gate_body, [thin, thin], [], 0, own_f, recv_f, bias_row, cot, after=(g_n,))
    g_fy = swap(g_f, "chan", 1)
    lanes = 3 * local_out

    def routed(mine_g, other_g):
        keep, send = jnp.where(x == y, mine_g, other_g), jnp.where(x == y, other_g, mine_g)
        return keep, send, swap(send, "slab", 2)

    keep_n, send_n, got_n = routed(g_n, g_ny)
    core_n = swap(keep_n, "slab", 1), swap(got_n, "slab", 1)
    keep_f, send_f, got_f = routed(g_f, g_fy)
    acc_shape = (3, 3 * local_in // 2, lanes)
    core_f = swap(keep_f, "slab", 1)
    sums_of = [(acc_shape, F32), ((8, lanes), F32)]
    four, two = pltpu.VMEM((4, padded, lanes), BF), pltpu.VMEM((2, padded, lanes), BF)
    first = functools.partial(first_kernel_body, ny)
    acc0, total0 = vmem_call(first, sums_of, [four], 2 * macs, vt, keep_n, core_n[0], keep_f, core_f)
    second = functools.partial(second_kernel_body, ny)
    acc0, total0 = vmem_call(second, sums_of, [two], macs, vt, got_n, core_n[1], acc0, total0)
    last_f = swap(held_back(got_f, total0[:, :local_out]), "slab", 1)
    single = pltpu.VMEM((1, padded, lanes), BF)
    acc1, total1 = vmem_call(
        functools.partial(next_kernel_body, 2, ny), sums_of, [single], macs, vt, got_f, acc0, total0
    )
    rows = 9 * local_in // 8
    cut = [((rows, lanes), F32), ((rows, lanes), BF), ((rows, lanes), F32), ((rows, lanes), BF)]
    if slabs == 4:
        keep, s1, s2, s3, total, sent = vmem_call(
            functools.partial(last_kernel_body, ny),
            cut + [((8, lanes), F32), thin],
            [single, pltpu.VMEM(acc_shape, F32)],
            macs,
            vt, last_f, acc1, total1, keep_f,
        )
    else:
        acc, total = vmem_call(
            functools.partial(next_kernel_body, 3, ny), sums_of, [single], macs, vt, last_f, acc1, total1
        )
        bit = 4
        while bit < slabs:
            acc, total = acc + swap(acc, "slab", bit), total + swap(total, "slab", bit)
            bit *= 2
        keep, s1, s2, s3 = vmem_call(cut_body, cut, [], 0, acc)
        sent = keep_f
    r3, r1, total_z2 = swap(s3, "dp", 1), swap(s1, "dp", 1), swap(total, "dp", 2)
    merged, total_a = (s2 + r3.astype(F32)).astype(BF), total + total_z2
    r2 = swap(merged, "dp", 2)

    sent_x = swap(sent, "slab", 2)
    wt = weight.reshape(27, local_in, outputs)
    ig_buf = pltpu.VMEM((3, padded, 3 * outputs), BF)
    ig_n, partial, act, ig_n_done = vmem_call(
        functools.partial(near_input_body, ny),
        [
            ((plane, local_in), BF), ((plane, local_in), F32), ((planes, plane, local_out), BF), ((8, lanes), F32)
        ],
        [ig_buf],
        2 * macs,
        keep_n, send_n, keep_f, send_f, core_n[0], swap(send_n, "slab", 1), wt, act_n, act_f,
        after=(merged, sent_x),
    )
    far_keep = last_f
    far_send = swap(sent_x, "slab", 1)
    if slabs > 4:
        edge = (mine == 0) | (mine == 3)
        far_keep = jnp.where(edge, next_pair(send_f), far_keep)
        far_send = jnp.where(edge, next_pair(keep_f), far_send)
    ig, ig_done = vmem_call(
        functools.partial(far_input_body, slabs == 4, ny),
        [((planes, plane, local_in), BF), ((8, lanes), F32)],
        [pltpu.VMEM((1, padded, 3 * outputs), BF)],
        0,
        far_keep, far_send, wt, partial, ig_n,
    )
    quarter = held_back(((keep + r1.astype(F32) + r2.astype(F32)) * factor).astype(BF), ig_n_done, total_z2)
    total_z1 = swap(total_a, "dp", 1)
    q1, q2, x0 = swap(quarter, "dp", 1), swap(quarter, "dp", 2), swap(quarter, "slab", 2)
    total_b = total_a + total_z1
    out_shape = (27, local_in, outputs)
    token = (((8, lanes), F32),)
    one_z, one_x, x0_z, four_c = vmem_call(
        round_body,
        [(quarter.shape, BF)] * 3 + [((4,) + quarter.shape, BF)],
        [],
        0,
        quarter, x0, q1, q2,
        after=(total_z1, ig_done),
    )
    q3, x2, x1, core = swap(one_z, "dp", 1), swap(one_x, "slab", 2), swap(x0_z, "dp", 1), swap(four_c, "slab", 1)
    last_x, two_c = vmem_call(
        next_round_body,
        [((rows + 16, lanes), BF), ((2,) + quarter.shape, BF)],
        [],
        0,
        core, q3, x2, total_b,
    )
    x3, core_b = swap(last_x, "slab", 2), swap(two_c, "slab", 1)
    out, done = spread(first_spread_body, out_shape, token, four_c, core, two_c)
    x3 = held_back(x3, done)
    pair_x = jnp.concatenate([x1, x3[:rows]], axis=0)
    core_x = swap(pair_x, "slab", 1)
    weight_grad = spread(last_spread_body, out_shape, (), pair_x, core_x, core_b, out, alias=True)[0]
    tail = x3[rows : rows + 1].astype(F32).reshape(3, local_out)
    bias_grad = jnp.where(x == y, total_b[0, :local_out], tail[0] + tail[1] + tail[2]) * factor
    shape = (samples, planes, nx, ny)
    return (
        act.reshape(shape + (local_out,)),
        ig.reshape(shape + (local_in,)),
        weight_grad.reshape(weight.shape),
        bias_grad,
    )


def group_ends(vol, slabs):
    before, after = jnp.zeros_like(vol[0]), jnp.zeros_like(vol[0])
    for group in range(4 if slabs > 4 else 0):
        up = [(i - 1, i + group) for i in range(4, slabs, 4)]
        down = [(i + 4, i + group) for i in range(0, slabs - 4, 4)]
        before = before + lax.ppermute(vol[vol.shape[0] - 1], "slab", up)
        after = after + lax.ppermute(vol[0], "slab", down)
    return jnp.stack([before, after])


def solution(mesh):
    placed = (
        P("dp", "slab", None, None, "chan"),
        P(None, None, None, "chan", None),
        P("chan"),
        P("dp", "slab", None, None, "chan"),
    )
    return jax.shard_map(
        per_device,
        mesh=mesh,
        in_specs=placed,
        out_specs=(
            P("dp", "slab", None, None, "chan"),
            P("dp", "slab", None, None, "chan"),
            P(None, None, None, "chan", None),
            P("chan"),
        ),
        check_vma=False,
    )
```
